512 devices in a mesh: occ: 64 (over y, z_hi, core), vir: 8 (over x, z_lo).
Axes of the slice: x: 4, y: 8, z: 8 (z_hi: 4, z_lo: 2; z = z_hi * 2 + z_lo), core: 2. Of those that a mesh axis runs over, the one named last changes fastest.
Arguments:
- amplitudes: bfloat16 [32768, 2048], P('occ'), may hold values from -6 to 6
- integrals: bfloat16 [2048, 12288], P('occ', 'vir'), may hold values from -0.1875 to 0.1875
- row_irreps: int32 [32], replicated, may hold values from 0 to 1, as said below
- column_irreps: int32 [192], P('vir'), may hold values from 0 to 1, as said below
- occ_energy: float32 [32768], P('occ'), may hold values from -1 to -0.3
- vir_energy: float32 [12288], P('vir'), may hold values from 0.5 to 2
Outputs:
- update: bfloat16 [32768, 12288], P('occ', 'vir')
The draws below stay inside these ranges and needn't reach their ends.
Inputs may be any that keep to these rules, and one draw needn't show every extreme that they name: `row_irreps`: each of the 2 labels is given to equally many cd tiles. `column_irreps`: each of the 2 labels is given to equally many ab tiles.
All inputs are finite; a program needn't handle non-finite values.
Results may differ from the reference program's by a relative error of at most 0.001.
Values may be sent and summed in bfloat16 or wider, within the bound.
A program may use at most 64 MiB of HBM per device.

```python
import jax
import jax.numpy as jnp
from jax import lax

TILE = 64
P_DEV = 512
KC = 2048
IRREPS = 2
PAIRS = 32768
AB = 12288
N_OCC = 64


def draw_row_irreps(key, part):
    key = jax.random.fold_in(key, 11)
    order = jax.random.permutation(key, KC // TILE)
    return (order % IRREPS).astype(jnp.int32)


def draw_column_irreps(key, part):
    key = jax.random.fold_in(key, 23)
    order = jax.random.permutation(key, AB // TILE)
    return (order % IRREPS).astype(jnp.int32)


def block_levels(key, shape, cuts, smallest, top_value):
    factor_of, own = 1.0, jax.random.fold_in(key, 6)
    for axis_at, shards_of in cuts:
        draws = jnp.exp(jax.random.uniform(jax.random.fold_in(own, axis_at), (shards_of,), jnp.float32, smallest / len(cuts), top_value / len(cuts)))
        factor_of = factor_of * jnp.repeat(draws, shape[axis_at] // shards_of).reshape([-1 if axis == axis_at else 1 for axis in range(len(shape))])
    return factor_of


def normal_values(key, shape, width, most, shards=(), held_as=jnp.bfloat16):
    values = jax.random.normal(key, shape, jnp.float32) * width
    if len(shards) > 0:
        values = block_levels(key, shape, shards, -0.22, 0.18) * values
    return jnp.clip(values, min=-most, max=most).astype(held_as)


def setup_inputs(seed: int = 0) -> dict:
    arg_keys = jax.random.split(jax.random.key(seed), 7)
    amplitudes = normal_values(arg_keys[0], (PAIRS, KC), 1.0, 6.0, ((0, 64),))
    integrals = normal_values(arg_keys[1], (KC, AB), (KC // 2) ** -0.5, 0.1875, ((0, 64), (1, 8)))
    row_irreps = draw_row_irreps(jax.random.fold_in(arg_keys[6], 71), 0)
    column_irreps = draw_column_irreps(jax.random.fold_in(arg_keys[6], 71), 0)
    occ_energy = jnp.clip(-1.0 + 0.7 * jax.random.uniform(arg_keys[4], (PAIRS,), jnp.float32) ** block_levels(arg_keys[4], (PAIRS,), ((0, 64),), -0.2, 0.2), -1.0, -0.3)
    vir_energy = jnp.clip(0.5 + 1.5 * jax.random.uniform(arg_keys[5], (AB,), jnp.float32) ** block_levels(arg_keys[5], (AB,), ((0, 8),), -0.2, 0.2), 0.5, 2.0)
    return dict(amplitudes=amplitudes, integrals=integrals, row_irreps=row_irreps, column_irreps=column_irreps, occ_energy=occ_energy, vir_energy=vir_energy)


def reference(amplitudes, integrals, row_irreps, column_irreps, occ_energy, vir_energy):
    row_labels = jnp.repeat(row_irreps, TILE)
    column_labels = jnp.repeat(column_irreps, TILE)
    masked = jnp.where(row_labels[:, None] == column_labels[None, :], integrals, jnp.zeros_like(integrals))
    blocks = amplitudes.reshape(N_OCC, P_DEV, KC)
    energies = occ_energy.reshape(N_OCC, P_DEV)
    half = N_OCC // 2

    def one_block(index):
        own_rows = blocks[index]
        mirrored = blocks[(index + half) % N_OCC]
        ladder = jnp.dot(own_rows, masked, preferred_element_type=jnp.float32) - jnp.dot(mirrored, masked, preferred_element_type=jnp.float32)
        denominator = vir_energy[None, :] - energies[index][:, None]
        return (ladder / denominator).astype(jnp.bfloat16)

    result = lax.map(one_block, jnp.arange(N_OCC, dtype=jnp.int32))
    return result.reshape(PAIRS, AB)
```

```python
import jax
import jax.numpy as jnp
from jax import lax
from jax.experimental import pallas as pl
from jax.experimental.pallas import tpu as pltpu
from jax.sharding import PartitionSpec as P

TILE = 64
MESH = pl.DeviceIdType.MESH
NY, NZ, NX = 8, 4, 4
Z_OFFSETS = (0, -1, 1, 2)
DELTAS = (0, 1, -1, 2, -2, 3, -3, 4)
N_SEMS = 96
ORDER = (
    ("z", 1), ("z", 2), ("relay", 1, 0), ("relay", -1, 0), ("y", 0, 1, 1), ("y", 0, 1, -1), ("zf", 0),
    ("y", 1, 1, 1), ("y", 1, 1, -1), ("own", 0), ("y", 2, 1, 1), ("y", 2, 1, -1), ("zf", -1),
    ("mir", 1, 0), ("mir", -1, 0), ("zf", 1), ("own", -1), ("y", 0, 2, 1), ("y", 0, 2, -1), ("own", 1),
    ("y", 1, 2, 1), ("y", 1, 2, -1), ("zl", 1, 0), ("x", 0, 1, 0, 1), ("x", 0, 1, 0, -1), ("y", 2, 2, 1),
    ("y", 2, 2, -1), ("zl", -1, 0), ("x", 0, -1, 0, 1), ("x", 0, -1, 0, -1), ("y", 0, 3, 1),
    ("y", 0, 3, -1), ("x", 1, 1, 0, 1), ("zf", -2), ("x", 1, 1, 0, -1), ("y", 1, 3, 1), ("y", 1, 3, -1),
    ("zf", 2), ("own", -2), ("y", 2, 3, 1), ("y", 2, 3, -1), ("xf", 0, 1, 0), ("x", 1, -1, 0, -1),
    ("y", 0, 4), ("y", 1, 4), ("own", 2), ("x", 1, -1, 0, 1), ("xf", 0, -1, 0), ("y", 2, 4), ("zf", -3),
    ("xf", 1, 1, 0), ("xf", 1, -1, 0), ("zf", 3), ("mirror", 0), ("mirror", 1), ("mirror", -1),
    ("mirror", 2), ("mirror", -2), ("zf", 4), ("full", 3), ("full", -3), ("full", 4),
)


def kernel(
    row_labels_hbm, column_labels_hbm, integrals_hbm, amplitudes, occ_energy_hbm, vir_energy_hbm, out,
    gathered, mirrored, relay, own, total, integrals, occ_energy, vir_rows, vir_energy, occ_column, row_labels, column_labels,
    send_sems, recv_sems, local_sems,
):
    occ, vir = lax.axis_index("occ"), lax.axis_index("vir")
    core = occ % 2
    zh = (occ // 2) % NZ
    y = occ // (2 * NZ)
    zl = vir % 2
    x = vir // 2

    def at(dy=0, dz=0, sibling=False):
        c = 1 - core if sibling else core
        return (((y + dy + NY) % NY) * NZ + (zh + dz + NZ) % NZ) * 2 + c

    def vir_at(dx=0, other=False):
        return ((x + dx + NX) % NX) * 2 + (1 - zl if other else zl)

    def slot(delta, stream, half=None, sibling=False):
        c = 1 - core if sibling else core
        ref = gathered.at[(y + delta + NY) % NY, (zh + Z_OFFSETS[stream] + NZ) % NZ, c]
        return ref if half is None else ref.at[pl.ds(16 * half, 16)]

    names = {}
    pending = []

    def sem_of(name):
        return names.setdefault(name, len(names))

    def send(name, source, target, to_occ=None, to_vir=None):
        k = sem_of(name)
        copy = pltpu.make_async_remote_copy(
            src_ref=source, dst_ref=target, send_sem=send_sems.at[k], recv_sem=recv_sems.at[k],
            device_id=(occ if to_occ is None else to_occ, vir if to_vir is None else to_vir),
            device_id_type=MESH,
        )
        copy.start()
        pending.append(copy)

    def arrived(name, target):
        k = sem_of(name)
        pltpu.make_async_remote_copy(
            src_ref=target, dst_ref=target, send_sem=send_sems.at[k], recv_sem=recv_sems.at[k],
            device_id=(at(sibling=True), vir), device_id_type=MESH,
        ).wait_recv()

    def half_of(distance, way):
        return None if distance < 4 else (0 if way > 0 else 1)

    def send_y(stream, distance, way):
        ref = slot(-way * (distance - 1), stream, half_of(distance, way))
        send(("y", stream, distance, way), ref, ref, to_occ=at(dy=way))

    def to_sibling(delta, stream):
        ref = slot(delta, stream)
        send(("sib", delta, stream), ref, ref, to_occ=at(sibling=True))

    def send_far(delta, stream):
        way = {1: 1, 2: -1}.get(stream)
        if way is not None:
            ref = slot(delta, stream, 0 if way > 0 else 1)
            send(("zf", delta, way), ref, ref, to_occ=at(dz=way))

    def start_stream(stream):
        send_y(stream, 1, 1)
        send_y(stream, 1, -1)
        to_sibling(0, stream)

    def on_z(stream):
        arrived(("z", stream), slot(0, stream))
        send_far(0, stream)
        start_stream(stream)

    def on_y(stream, distance, way=None):
        for w in (1, -1) if way is None else (way,):
            arrived(("y", stream, distance, w), slot(-w * distance, stream, half_of(distance, w)))
        if distance < 4:
            send_y(stream, distance + 1, way)
            send_far(-way * distance, stream)
            to_sibling(-way * distance, stream)
        else:
            send_far(4, stream)
            to_sibling(4, stream)

    def on_zf(delta):
        for way in (1, -1):
            arrived(("zf", delta, way), slot(delta, 3, 0 if way > 0 else 1))
        to_sibling(delta, 3)

    def piece(dx, other, way):
        return mirrored.at[vir_at(dx, other), 0 if way > 0 else 1]

    def on_relay(way, _):
        ref = relay.at[0 if way > 0 else 1]
        arrived(("relay", way), ref)
        send(("mir", way), ref, piece(0, False, way), to_occ=at(dy=2 * way))

    def to_x(other, way):
        ref = piece(0, other, way)
        for w in (1, -1):
            send(("x", other, way, w), ref, ref, to_vir=vir_at(w))

    def on_mir(way, _):
        ref = piece(0, False, way)
        arrived(("mir", way), ref)
        send(("zl", way), ref, ref, to_vir=vir_at(0, True))
        to_x(0, way)

    def on_zl(way, _):
        arrived(("zl", way), piece(0, True, way))
        to_x(1, way)

    def on_x(other, way, _, w):
        ref = piece(-w, other, way)
        arrived(("x", other, way, w), ref)
        if w == way:
            send(("xf", other, way), ref, ref, to_vir=vir_at(w))

    def on_xf(other, way, _):
        arrived(("xf", other, way), piece(2, other, way))

    started = []

    def chunk(delta, with_own, with_mirrored, last=False):
        first = not started
        started.append(delta)
        block = (y + delta + NY) % NY
        depth = pl.ds(pl.multiple_of(block * 256, 256), 256)

        @pl.loop(0, 6)
        def _(n):
            columns = pl.ds(pl.multiple_of(n * 256, 256), 256)
            g = gathered[block, :, :, :, columns].reshape(256, 256)
            value = None if first else total[:, columns]
            if with_own:
                term = jnp.dot(own[:, depth], g, preferred_element_type=jnp.float32)
                value = term if value is None else value + term
            if with_mirrored:
                a = mirrored[:, :, :, depth].reshape(512, 256)
                value = value - jnp.dot(a, g, preferred_element_type=jnp.float32)
            if last:
                out[:, columns] = (value / (vir_energy[n] - occ_column[...])).astype(jnp.bfloat16)
            else:
                total[:, columns] = value

    def wait_chunk(delta):
        for stream in range(4):
            arrived(("sib", delta, stream), slot(delta, stream, sibling=True))

    def on_own(delta):
        wait_chunk(delta)
        if not started:
            own_copy.wait()
        chunk(delta, True, False)

    def on_mirror(delta):
        chunk(delta, False, True)

    def on_full(delta):
        wait_chunk(delta)
        chunk(delta, True, True, last=delta == 4)

    def local(source, target, k):
        copy = pltpu.make_async_copy(source, target, local_sems.at[k])
        copy.start()
        return copy

    small = [
        local(row_labels_hbm, row_labels, 0),
        local(column_labels_hbm, column_labels, 1),
        local(integrals_hbm, integrals, 2),
        local(occ_energy_hbm, occ_energy, 3),
        local(vir_energy_hbm, vir_rows, 4),
    ]
    own_copy = local(amplitudes, own, 5)

    barrier = pltpu.get_barrier_semaphore()
    peers = [(at(dy=d), vir) for d in (1, -1, 2, -2)] + [(at(dz=d), vir) for d in (1, -1)]
    peers += [(at(sibling=True), vir), (occ, vir_at(0, True)), (occ, vir_at(1)), (occ, vir_at(-1))]
    for peer in peers:
        pl.semaphore_signal(barrier, inc=1, device_id=peer, device_id_type=MESH)

    for copy in small:
        copy.wait()
    tile_of = lax.broadcasted_iota(jnp.int32, (1, 24 * TILE), 1) // TILE
    labels = jnp.zeros((1, 24 * TILE), jnp.int32)
    for t in range(24):
        labels = jnp.where(tile_of == t, column_labels[t], labels)
    keep = jnp.broadcast_to(labels == row_labels[occ // 2], (32, 24 * TILE))
    gathered[y, zh, core] = jnp.where(keep, integrals[...].astype(jnp.float32), 0.0).astype(jnp.bfloat16)

    pl.semaphore_wait(barrier, len(peers))

    for way in (1, -1):
        half = 0 if way > 0 else 1
        rows = pl.ds(pl.multiple_of(vir * 64 + 32 * half, 32), 32)
        send(("relay", way), amplitudes.at[rows], relay.at[half], to_occ=at(dy=2 * way))
    send(("z", 1), slot(0, 0), slot(0, 0), to_occ=at(dz=1))
    send(("z", 2), slot(0, 0), slot(0, 0), to_occ=at(dz=-1))
    start_stream(0)
    for t in range(12):
        vir_energy[t // 2, :, 128 * (t % 2) : 128 * (t % 2) + 128] = vir_rows[t : t + 1, :]
    for b in range(4):
        block = jnp.transpose(jnp.broadcast_to(occ_energy[b : b + 1, :], (128, 128)))
        occ_column[128 * b : 128 * b + 128, :] = jnp.concatenate([block, block], axis=1)

    handlers = {
        "z": on_z, "y": on_y, "zf": on_zf, "relay": on_relay, "mir": on_mir, "zl": on_zl, "x": on_x, "xf": on_xf,
        "own": on_own, "mirror": on_mirror, "full": on_full,
    }
    for kind, *place in ORDER:
        handlers[kind](*place)
    for copy in pending:
        copy.wait_send()


def body(amplitudes, integrals, row_irreps, column_irreps, occ_energy, vir_energy):
    hbm = pl.BlockSpec(memory_space=pltpu.HBM)
    return pl.pallas_call(
        kernel,
        out_shape=pltpu.VMEM((512, 1536), jnp.bfloat16),
        in_specs=[hbm] * 6,
        out_specs=pl.BlockSpec(memory_space=pltpu.VMEM),
        scratch_shapes=[
            pltpu.VMEM((NY, NZ, 2, 32, 1536), jnp.bfloat16),
            pltpu.VMEM((8, 2, 32, 2048), jnp.bfloat16),
            pltpu.VMEM((2, 32, 2048), jnp.bfloat16),
            pltpu.VMEM((512, 2048), jnp.bfloat16),
            pltpu.VMEM((512, 1536), jnp.float32),
            pltpu.VMEM((32, 1536), jnp.bfloat16),
            pltpu.VMEM((4, 128), jnp.float32),
            pltpu.VMEM((12, 128), jnp.float32),
            pltpu.VMEM((6, 1, 256), jnp.float32),
            pltpu.VMEM((512, 256), jnp.float32),
            pltpu.SMEM((32,), jnp.int32),
            pltpu.SMEM((24,), jnp.int32),
            pltpu.SemaphoreType.DMA((N_SEMS,)),
            pltpu.SemaphoreType.DMA((N_SEMS,)),
            pltpu.SemaphoreType.DMA((6,)),
        ],
        compiler_params=pltpu.CompilerParams(
            collective_id=0, has_side_effects=True, vmem_limit_bytes=58 * 2**20
        ),
        cost_estimate=pl.CostEstimate(flops=6442450944, bytes_accessed=4 * 2**20, transcendentals=0),
    )(
        row_irreps, column_irreps, integrals, amplitudes,
        occ_energy.reshape(4, 128), vir_energy.reshape(12, 128),
    )


def solution(mesh):
    placed = (P("occ", None), P("occ", "vir"), P(), P("vir"), P("occ"), P("vir"))
    return jax.shard_map(
        body, mesh=mesh, in_specs=placed, out_specs=P("occ", "vir"), check_vma=False
    )
```

```python
import jax
import jax.numpy as jnp
from jax import lax
from jax.experimental import pallas as pl
from jax.experimental.pallas import tpu as pltpu
from jax.sharding import PartitionSpec as P

TILE = 64
MESH = pl.DeviceIdType.MESH
NY, NZ, NX = 8, 4, 4
DELTAS = (0, 1, -1, 2, -2, 3, -3, 4)
N_SEMS = 128
ORDER = (
    ("a1",), ("inverse",), ("mir", 1, 0), ("mir", -1, 0), ("a2",), ("zl", 1, 0), ("x", 0, 1, 0, 1),
    ("x", 0, 1, 0, -1), ("zl", -1, 0), ("x", 0, -1, 0, 1), ("x", 0, -1, 0, -1), ("z", 1), ("z", 3),
    ("x", 1, 1, 0, 1), ("x", 1, 1, 0, -1), ("mir", 1, 1), ("mir", -1, 1), ("xf", 0, 1, 0),
    ("x", 1, -1, 0, -1), ("y", 0, 1, 1), ("y", 0, 1, -1), ("x", 1, -1, 0, 1), ("xf", 0, -1, 0),
    ("y", 1, 1, 1), ("y", 1, 1, -1), ("zf",), ("y", 3, 1, 1), ("y", 3, 1, -1), ("xf", 1, 1, 0),
    ("x", 0, 1, 1, -1), ("zl", 1, 1), ("y", 0, 2, 1), ("y", 0, 2, -1), ("x", 0, 1, 1, 1),
    ("x", 0, -1, 1, -1), ("zl", -1, 1), ("y", 1, 2, 1), ("y", 1, 2, -1), ("x", 0, -1, 1, 1),
    ("xf", 1, -1, 0), ("y", 2, 1, 1), ("y", 2, 1, -1), ("y", 3, 2, 1), ("y", 3, 2, -1), ("x", 1, 1, 1, 1),
    ("x", 1, 1, 1, -1), ("y", 0, 3, 1), ("y", 0, 3, -1), ("unpack", 0), ("xf", 0, 1, 1), ("xf", 0, -1, 1),
    ("own", 0), ("y", 1, 3, 1), ("y", 1, 3, -1), ("x", 1, -1, 1, 1), ("x", 1, -1, 1, -1), ("y", 2, 2, 1),
    ("y", 2, 2, -1), ("y", 3, 3, 1), ("y", 3, 3, -1), ("xf", 1, 1, 1), ("y", 0, 4), ("unpack", 1),
    ("y", 1, 4), ("own", 1), ("y", 2, 3, 1), ("xf", 1, -1, 1), ("y", 2, 3, -1), ("y", 3, 4), ("mirror", 0),
    ("mirror", 1), ("y", 2, 4), ("unpack", 2), ("own", 2), ("mirror", 2), ("unpack", 3), ("own", 3),
    ("mirror", 3),
)


def kernel(
    row_labels_hbm, column_labels_hbm, integrals, amplitudes, occ_energy_hbm, vir_energy_hbm, out,
    packed_0, packed_1, packed_2, packed_3, packed_4, packed_5, packed_6, packed_7,
    first, second, mirrored, own, masked, total, inverse, occ_energy, vir_energy, occ_column, masks,
    order_vmem, order, ranks, row_labels, column_labels, send_sems, recv_sems, local_sems,
):
    packed = dict(zip(DELTAS, (packed_0, packed_1, packed_2, packed_3, packed_4, packed_5, packed_6, packed_7)))
    occ, vir = lax.axis_index("occ"), lax.axis_index("vir")
    core = occ % 2
    zh = (occ // 2) % NZ
    y = occ // (2 * NZ)
    zl = vir % 2
    x = vir // 2
    owner = zh != 3

    def at(dy=0, dz=0, sibling=False):
        c = 1 - core if sibling else core
        return (((y + dy + NY) % NY) * NZ + (zh + dz + NZ) % NZ) * 2 + c

    def vir_at(dx=0, other=False):
        return ((x + dx + NX) % NX) * 2 + (1 - zl if other else zl)

    def valid(stream):
        return (zh + stream) % NZ != 3

    names = {}
    pending = []

    def sem_of(name):
        return names.setdefault(name, len(names))

    def send(name, source, target, to_occ=None, to_vir=None, when=None):
        k = sem_of(name)

        def descriptor():
            return pltpu.make_async_remote_copy(
                src_ref=source(), dst_ref=target(), send_sem=send_sems.at[k], recv_sem=recv_sems.at[k],
                device_id=(occ if to_occ is None else to_occ, vir if to_vir is None else to_vir),
                device_id_type=MESH,
            )

        if when is None:
            descriptor().start()
            pending.append(lambda: descriptor().wait_send())
        else:
            pl.when(when)(lambda: descriptor().start())
            pending.append(lambda: pl.when(when)(lambda: descriptor().wait_send()))

    def arrived(name, target, when=None):
        k = sem_of(name)

        def wait():
            pltpu.make_async_remote_copy(
                src_ref=target(), dst_ref=target(), send_sem=send_sems.at[k], recv_sem=recv_sems.at[k],
                device_id=(at(sibling=True), vir), device_id_type=MESH,
            ).wait_recv()

        if when is None:
            wait()
        else:
            pl.when(when)(wait)

    def columns_of(t):
        return pl.ds(pl.multiple_of(512 * t, 512), 512)

    def send_first():
        for s in (1, 3, 2):
            t = (zh + s) % NZ
            send(("first", s), lambda t=t: integrals.at[:, columns_of(t)], lambda: first.at[zh], at(dz=s), when=t != 3)

    def unit(plane):
        rows = pl.ds(pl.multiple_of(16 * (plane % 2), 16), 16)
        return first.at[:, rows, pl.ds(pl.multiple_of(128 * (plane // 2), 128), 128)]

    def second_from(plane):
        return second.at[pl.ds(pl.multiple_of(4 * plane, 4), 4)]

    def on_first():
        for s in (1, 3, 2):
            arrived(("first", s), lambda s=s: first.at[(zh - s + NZ) % NZ], when=owner)

        @pl.when(owner)
        def _():
            pltpu.make_async_copy(integrals.at[:, columns_of(zh)], first.at[zh], local_sems.at[6]).wait()
            pltpu.make_async_copy(unit(y), second_from(y), local_sems.at[7]).start()

        for d in (4, 3, -3, 2, -2, 1, -1):
            plane = (y + d + NY) % NY
            send(("second", d), lambda p=plane: unit(p), lambda: second_from(y), at(dy=d), when=owner)
        for way in (1, -1):
            send_mirror(way, 1)

    def on_second():
        for d in (1, -1, 2, -2, 3, -3, 4):
            arrived(("second", d), lambda d=d: second_from((y - d + NY) % NY), when=owner)

        @pl.when(owner)
        def _():
            pltpu.make_async_copy(unit(y), second_from(y), local_sems.at[7]).wait()
            zero = masks[0, 4 * zh + y // 2].astype(jnp.float32) > 0.5

            @pl.loop(0, 16)
            def _(p):
                a = second[order[0, p]].astype(jnp.float32)
                b = second[order[0, 16 + p]].astype(jnp.float32)
                packed[0][0, core, p] = jnp.where(zero, a, b).astype(jnp.bfloat16)

        for s in (3, 1):
            send(("z", s), slot(0, 0), slot(0, s), at(dz=-s), when=owner)
        start_stream(0)

    def slot(delta, stream, half=None, sibling=False):
        def ref():
            r = packed[delta].at[stream, 1 - core if sibling else core]
            return r if half is None else r.at[pl.ds(8 * half, 8)]

        return ref

    def half_of(distance, way):
        return None if distance < 4 else (0 if way > 0 else 1)

    def delta_of(distance, way):
        return 4 if distance == 4 else -way * distance

    def send_y(stream, distance, way):
        half = half_of(distance, way)
        source = slot(delta_of(distance - 1, way), stream, half)
        target = slot(delta_of(distance, way), stream, half)
        send(("y", stream, distance, way), source, target, at(dy=way), when=valid(stream))

    def to_sibling(delta, stream):
        ref = slot(delta, stream)
        send(("sib", delta, stream), ref, ref, at(sibling=True), when=valid(stream))

    def start_stream(stream):
        send_y(stream, 1, 1)
        send_y(stream, 1, -1)
        to_sibling(0, stream)

    def on_z(stream):
        arrived(("z", stream), slot(0, stream), when=valid(stream))
        way = 1 if stream == 3 else -1
        half = 0 if way > 0 else 1
        send(("zf", half), slot(0, stream, half), slot(0, 2, half), at(dz=way), when=valid(stream))
        start_stream(stream)

    def on_zf():
        for half in (0, 1):
            arrived(("zf", half), slot(0, 2, half), when=valid(2))
        start_stream(2)

    def on_y(stream, distance, way=None):
        for w in (1, -1) if way is None else (way,):
            ref = slot(delta_of(distance, w), stream, half_of(distance, w))
            arrived(("y", stream, distance, w), ref, when=valid(stream))
        if distance < 4:
            send_y(stream, distance + 1, way)
        to_sibling(delta_of(distance, way), stream)

    def index_of(way, part):
        return part + (0 if way > 0 else 2)

    def piece(dx, other, way, part):
        return lambda: mirrored.at[vir_at(dx, other), index_of(way, part)]

    def send_mirror(way, part):
        rows = pl.ds(pl.multiple_of(vir * 64 + 16 * index_of(way, part), 16), 16)
        send(("mir", way, part), lambda: amplitudes.at[rows], piece(0, False, way, part), at(dy=4))

    def to_x(other, way, part):
        ref = piece(0, other, way, part)
        for w in (1, -1):
            send(("x", other, way, part, w), ref, ref, to_vir=vir_at(w))

    def on_mir(way, part):
        ref = piece(0, False, way, part)
        arrived(("mir", way, part), ref)
        send(("zl", way, part), ref, ref, to_vir=vir_at(0, True))
        to_x(0, way, part)

    def on_zl(way, part):
        arrived(("zl", way, part), piece(0, True, way, part))
        to_x(1, way, part)

    def on_x(other, way, part, w):
        ref = piece(-w, other, way, part)
        arrived(("x", other, way, part, w), ref)
        if w == way:
            send(("xf", other, way, part), ref, ref, to_vir=vir_at(w))

    def on_xf(other, way, part):
        arrived(("xf", other, way, part), piece(2, other, way, part))

    odd = y % 2
    groups = (
        (((0, 0), (1, 1)), ((0, -1), (1, 0)), 0, 0),
        (((0, -2), (1, -1)), ((0, 1), (1, 2)), -1, 1),
        (((0, 2), (1, 3)), ((0, -3), (1, -2)), 1, -1),
        (((0, 4), (1, -3)), ((0, 3), (1, 4)), 2, 2),
    )
    needs = ((0, 1, -1), (2, -2), (3, -3), (4,))

    def group_of(k):
        return (y // 2 + jnp.where(odd == 1, groups[k][3], groups[k][2]) + 4) % 4

    def unpack(k):
        group = group_of(k)

        def fill(planes):
            @pl.loop(0, 32)
            def _(r):
                label, rank = row_labels[r], ranks[r]
                for t in range(3):
                    keep = masks[label, 4 * t + group]
                    for parity, delta in planes:
                        for c in range(2):
                            rows = pl.ds(pl.multiple_of(r * 64 + 16 * (2 * c + parity), 16), 16)
                            value = packed[delta][(t - zh + NZ) % NZ, c, rank]
                            masked[k, rows, 128 * t : 128 * t + 128] = value * keep

        pl.when(odd == 0)(lambda: fill(groups[k][0]))
        pl.when(odd == 1)(lambda: fill(groups[k][1]))

    def own_part(k):
        return jnp.dot(own[...], masked[k], preferred_element_type=jnp.float32)

    def finish(k, value):
        group = group_of(k)
        a = mirrored[...].reshape(512, 2048)
        value = value - jnp.dot(a, masked[k], preferred_element_type=jnp.float32)
        for t in range(3):
            place = 4 * t + group
            columns = pl.ds(pl.multiple_of(128 * place, 128), 128)
            out[:, columns] = (value[:, 128 * t : 128 * t + 128] * inverse[place]).astype(jnp.bfloat16)

    def on_inverse():
        @pl.loop(0, 12)
        def _(t):
            inverse[t] = 1.0 / (vir_energy[pl.ds(t, 1), :] - occ_column[...])

    def on_unpack(k):
        for delta in needs[k]:
            for s in range(4):
                arrived(("sib", delta, s), slot(delta, s, sibling=True), when=valid(s))
        if k == 0:
            own_copy.wait()
        unpack(k)

    def on_own(k):
        total[k] = own_part(k)

    def on_mirror(k):
        finish(k, total[k])

    def local(source, target, k):
        copy = pltpu.make_async_copy(source, target, local_sems.at[k])
        copy.start()
        return copy

    labels_copies = [local(row_labels_hbm, row_labels, 0), local(column_labels_hbm, column_labels, 1)]
    energy_copies = [local(occ_energy_hbm, occ_energy, 3), local(vir_energy_hbm, vir_energy, 4)]
    own_copy = local(amplitudes, own, 5)

    @pl.when(owner)
    def _():
        pltpu.make_async_copy(integrals.at[:, columns_of(zh)], first.at[zh], local_sems.at[6]).start()

    barrier = pltpu.get_barrier_semaphore()
    peers = [(at(dy=d), vir) for d in (1, -1, 2, -2, 3, -3, 4)] + [(at(dz=d), vir) for d in (1, -1, 2)]
    peers += [(at(sibling=True), vir), (occ, vir_at(0, True)), (occ, vir_at(1)), (occ, vir_at(-1))]
    for peer in peers:
        pl.semaphore_signal(barrier, inc=1, device_id=peer, device_id_type=MESH)
    pl.semaphore_wait(barrier, len(peers))

    send_first()
    for way in (1, -1):
        send_mirror(way, 0)

    for copy in labels_copies:
        copy.wait()
    lane = lax.broadcasted_iota(jnp.int32, (8, 128), 1)
    places = jnp.zeros((8, 128), jnp.int32)
    ones = jnp.int32(0)
    for r in range(32):
        label = row_labels[r]
        rank = jnp.minimum(jnp.where(label == 1, ones, r - ones), 15)
        ranks[r] = rank
        places = jnp.where(lane == label * 16 + rank, r, places)
        ones = ones + label
    order_vmem[...] = places
    order_copy = local(order_vmem, order, 2)

    side = lax.broadcasted_iota(jnp.int32, (16, 128), 1) < TILE
    for t in range(12):
        label = jnp.where(side, column_labels[2 * t], column_labels[2 * t + 1])
        for value in (0, 1):
            masks[value, t] = jnp.where(label == value, 1.0, 0.0).astype(jnp.bfloat16)
    for copy in energy_copies:
        copy.wait()
    for b in range(4):
        occ_column[128 * b : 128 * b + 128, :] = jnp.transpose(
            jnp.broadcast_to(occ_energy[b : b + 1, :], (128, 128))
        )
    order_copy.wait()

    handlers = {
        "a1": on_first, "a2": on_second, "z": on_z, "y": on_y, "zf": on_zf, "mir": on_mir, "zl": on_zl,
        "x": on_x, "xf": on_xf, "inverse": on_inverse, "unpack": on_unpack, "own": on_own, "mirror": on_mirror,
    }
    for kind, *place in ORDER:
        handlers[kind](*place)
    for wait in pending:
        wait()


def body(amplitudes, integrals, row_irreps, column_irreps, occ_energy, vir_energy):
    hbm = pl.BlockSpec(memory_space=pltpu.HBM)
    return pl.pallas_call(
        kernel,
        out_shape=pltpu.VMEM((512, 1536), jnp.bfloat16),
        in_specs=[hbm] * 6,
        out_specs=pl.BlockSpec(memory_space=pltpu.VMEM),
        scratch_shapes=[pltpu.VMEM((4, 2, 16, 16, 128), jnp.bfloat16)] * 8
        + [
            pltpu.VMEM((4, 32, 512), jnp.bfloat16),
            pltpu.VMEM((32, 16, 128), jnp.bfloat16),
            pltpu.VMEM((8, 4, 16, 2048), jnp.bfloat16),
            pltpu.VMEM((512, 2048), jnp.bfloat16),
            pltpu.VMEM((4, 2048, 384), jnp.bfloat16),
            pltpu.VMEM((4, 512, 384), jnp.float32),
            pltpu.VMEM((12, 512, 128), jnp.float32),
            pltpu.VMEM((4, 128), jnp.float32),
            pltpu.VMEM((12, 128), jnp.float32),
            pltpu.VMEM((512, 128), jnp.float32),
            pltpu.VMEM((2, 12, 16, 128), jnp.bfloat16),
            pltpu.VMEM((8, 128), jnp.int32),
            pltpu.SMEM((8, 128), jnp.int32),
            pltpu.SMEM((32,), jnp.int32),
            pltpu.SMEM((32,), jnp.int32),
            pltpu.SMEM((24,), jnp.int32),
            pltpu.SemaphoreType.DMA((N_SEMS,)),
            pltpu.SemaphoreType.DMA((N_SEMS,)),
            pltpu.SemaphoreType.DMA((8,)),
        ],
        compiler_params=pltpu.CompilerParams(
            collective_id=0, has_side_effects=True, vmem_limit_bytes=58 * 2**20
        ),
        cost_estimate=pl.CostEstimate(flops=6442450944, bytes_accessed=4 * 2**20, transcendentals=0),
    )(
        row_irreps, column_irreps, integrals, amplitudes,
        occ_energy.reshape(4, 128), vir_energy.reshape(12, 128),
    )


def solution(mesh):
    placed = (P("occ", None), P("occ", "vir"), P(), P("vir"), P("occ"), P("vir"))
    return jax.shard_map(
        body, mesh=mesh, in_specs=placed, out_specs=P("occ", "vir"), check_vma=False
    )
```

```python
import jax
import jax.numpy as jnp
from jax import lax
from jax.experimental import pallas as pl
from jax.experimental.pallas import tpu as pltpu
from jax.sharding import PartitionSpec as P

TILE = 64
MESH = pl.DeviceIdType.MESH
NY, NZ, NX = 8, 4, 4
DELTAS = (0, 1, -1, 2, -2, 3, -3, 4)
N_SEMS = 128
ORDER = (
    ("sort",), ("a1",), ("inverse",), ("relay", 1, 0), ("relay", -1, 0), ("a2",), ("relay", 1, 1), ("relay", -1, 1),
    ("z", 3), ("z", 1), ("mir", 1, 0), ("mir", -1, 0), ("y", 0, 1, 1), ("y", 0, 1, -1), ("zf",),
    ("x", 0, 1, 0, 1), ("x", 0, 1, 0, -1), ("zl", 1, 0), ("mir", 1, 1), ("mir", -1, 1), ("y", 3, 1, 1),
    ("x", 0, -1, 0, 1), ("x", 0, -1, 0, -1), ("y", 3, 1, -1), ("zl", -1, 0), ("y", 1, 1, 1),
    ("y", 1, 1, -1), ("y", 0, 2, 1), ("xf", 0, 1, 0), ("y", 0, 2, -1), ("x", 1, 1, 0, -1), ("zl", 1, 1),
    ("y", 2, 1, 1), ("y", 2, 1, -1), ("x", 1, 1, 0, 1), ("x", 0, 1, 1, -1), ("zl", -1, 1), ("y", 3, 2, 1),
    ("y", 3, 2, -1), ("x", 0, 1, 1, 1), ("x", 0, -1, 1, -1), ("y", 1, 2, 1), ("y", 1, 2, -1), ("own", 0),
    ("y", 0, 3, 1), ("x", 0, -1, 1, 1), ("y", 0, 3, -1), ("xf", 0, -1, 0), ("y", 2, 2, 1), ("y", 2, 2, -1),
    ("x", 1, -1, 0, 1), ("x", 1, -1, 0, -1), ("y", 3, 3, 1), ("y", 3, 3, -1), ("x", 1, 1, 1, 1),
    ("x", 1, 1, 1, -1), ("y", 1, 3, 1), ("y", 1, 3, -1), ("own", 1), ("y", 0, 4), ("xf", 1, 1, 0),
    ("x", 1, -1, 1, -1), ("y", 2, 3, 1), ("y", 2, 3, -1), ("y", 3, 4), ("x", 1, -1, 1, 1),
    ("xf", 0, -1, 1), ("y", 1, 4), ("xf", 0, 1, 1), ("own", 2), ("xf", 1, -1, 0), ("y", 2, 4),
    ("xf", 1, 1, 1), ("xf", 1, -1, 1), ("mirror", 0), ("mirror", 1), ("mirror", 2), ("own", 3),
    ("mirror", 3),
)


def kernel(
    row_labels_hbm, column_labels_hbm, integrals, amplitudes, occ_energy_hbm, vir_energy_hbm, out,
    packed, mirrored, plain, own, total, inverse, first, second, relay, occ_energy, vir_energy, occ_column, zeros,
    order_vmem, order, row_labels, column_labels, send_sems, recv_sems, local_sems,
):
    occ, vir = lax.axis_index("occ"), lax.axis_index("vir")
    core = occ % 2
    zh = (occ // 2) % NZ
    y = occ // (2 * NZ)
    zl = vir % 2
    x = vir // 2
    owner = zh != 3

    def at(dy=0, dz=0, sibling=False):
        c = 1 - core if sibling else core
        return (((y + dy + NY) % NY) * NZ + (zh + dz + NZ) % NZ) * 2 + c

    def vir_at(dx=0, other=False):
        return ((x + dx + NX) % NX) * 2 + (1 - zl if other else zl)

    def valid(stream):
        return (zh + stream) % NZ != 3

    names = {}
    pending = []

    def sem_of(name):
        return names.setdefault(name, len(names))

    def send(name, source, target, to_occ=None, to_vir=None, when=None):
        k = sem_of(name)

        def descriptor():
            return pltpu.make_async_remote_copy(
                src_ref=source(), dst_ref=target(), send_sem=send_sems.at[k], recv_sem=recv_sems.at[k],
                device_id=(occ if to_occ is None else to_occ, vir if to_vir is None else to_vir),
                device_id_type=MESH,
            )

        if when is None:
            descriptor().start()
            pending.append(lambda: descriptor().wait_send())
        else:
            pl.when(when)(lambda: descriptor().start())
            pending.append(lambda: pl.when(when)(lambda: descriptor().wait_send()))

    def arrived(name, target, when=None):
        k = sem_of(name)

        def wait():
            pltpu.make_async_remote_copy(
                src_ref=target(), dst_ref=target(), send_sem=send_sems.at[k], recv_sem=recv_sems.at[k],
                device_id=(at(sibling=True), vir), device_id_type=MESH,
            ).wait_recv()

        if when is None:
            wait()
        else:
            pl.when(when)(wait)

    def columns_of(t):
        return pl.ds(pl.multiple_of(512 * t, 512), 512)

    def send_first():
        for s in (1, 3, 2):
            t = (zh + s) % NZ
            send(("first", s), lambda t=t: integrals.at[:, columns_of(t)], lambda: first.at[zh], at(dz=s), when=t != 3)

    def unit(plane):
        rows = pl.ds(pl.multiple_of(16 * (plane % 2), 16), 16)
        return first.at[:, rows, pl.ds(pl.multiple_of(128 * (plane // 2), 128), 128)]

    def second_from(plane):
        return second.at[pl.ds(pl.multiple_of(4 * plane, 4), 4)]

    def on_first():
        for s in (1, 3, 2):
            arrived(("first", s), lambda s=s: first.at[(zh - s + NZ) % NZ], when=owner)

        @pl.when(owner)
        def _():
            pltpu.make_async_copy(integrals.at[:, columns_of(zh)], first.at[zh], local_sems.at[6]).wait()
            pltpu.make_async_copy(unit(y), second_from(y), local_sems.at[7]).start()

        for d in (4, 3, -3, 2, -2, 1, -1):
            plane = (y + d + NY) % NY
            send(("second", d), lambda p=plane: unit(p), lambda: second_from(y), at(dy=d), when=owner)
        for way in (1, -1):
            send_mirror(way, 1)

    def on_second():
        for d in (1, -1, 2, -2, 3, -3, 4):
            arrived(("second", d), lambda d=d: second_from((y - d + NY) % NY), when=owner)

        @pl.when(owner)
        def _():
            pltpu.make_async_copy(unit(y), second_from(y), local_sems.at[7]).wait()
            zero = jnp.broadcast_to(zeros[4 * zh + y // 2], (16, 128)) == 1
            columns = pl.ds(pl.multiple_of(128 * (4 * zh + y // 2), 128), 128)

            @pl.loop(0, 16)
            def _(p):
                a = second[order[0, p]].astype(jnp.float32)
                b = second[order[0, 16 + p]].astype(jnp.float32)
                packed[p, 2 * core + y % 2, :, columns] = jnp.where(zero, a, b).astype(jnp.bfloat16)

        for s in (3, 1):
            send(("z", s), slot(0, 0), slot(0, 0), at(dz=-s), when=owner)
        start_stream(0)

    def slot(delta, stream, half=None, sibling=False):
        def ref():
            plane, block = (y + delta + NY) % NY, (zh + stream) % NZ
            rows = slice(None) if half is None else pl.ds(8 * half, 8)
            columns = pl.ds(pl.multiple_of(128 * (4 * block + plane // 2), 128), 128)
            c = 1 - core if sibling else core
            return packed.at[rows, 2 * c + plane % 2, :, columns]

        return ref

    def half_of(distance, way):
        return None if distance < 4 else (0 if way > 0 else 1)

    def delta_of(distance, way):
        return 4 if distance == 4 else -way * distance

    def send_y(stream, distance, way):
        half = half_of(distance, way)
        ref = slot(delta_of(distance - 1, way), stream, half)
        send(("y", stream, distance, way), ref, ref, at(dy=way), when=valid(stream))

    def to_sibling(delta, stream):
        ref = slot(delta, stream)
        send(("sib", delta, stream), ref, ref, at(sibling=True), when=valid(stream))

    def start_stream(stream):
        send_y(stream, 1, 1)
        send_y(stream, 1, -1)
        to_sibling(0, stream)

    def on_z(stream):
        arrived(("z", stream), slot(0, stream), when=valid(stream))
        way = 1 if stream == 3 else -1
        half = 0 if way > 0 else 1
        ref = slot(0, stream, half)
        send(("zf", half), ref, ref, at(dz=way), when=valid(stream))
        start_stream(stream)

    def on_zf():
        for half in (0, 1):
            arrived(("zf", half), slot(0, 2, half), when=valid(2))
        start_stream(2)

    def on_y(stream, distance, way=None):
        for w in (1, -1) if way is None else (way,):
            ref = slot(delta_of(distance, w), stream, half_of(distance, w))
            arrived(("y", stream, distance, w), ref, when=valid(stream))
        if distance < 4:
            send_y(stream, distance + 1, way)
        to_sibling(delta_of(distance, way), stream)

    def index_of(way, part):
        return part + (0 if way > 0 else 2)

    def piece(dx, other, way, part):
        return lambda: mirrored.at[vir_at(dx, other), index_of(way, part)]

    def relay_of(way, part):
        return lambda: relay.at[index_of(way, part)]

    def send_mirror(way, part):
        rows = pl.ds(pl.multiple_of(vir * 64 + 16 * index_of(way, part), 16), 16)
        send(("relay", way, part), lambda: own.at[rows], relay_of(way, part), at(dy=2 * way))

    def on_relay(way, part):
        arrived(("relay", way, part), relay_of(way, part))
        send(("mir", way, part), relay_of(way, part), piece(0, False, way, part), at(dy=2 * way))

    def to_x(other, way, part):
        ref = piece(0, other, way, part)
        for w in (1, -1):
            send(("x", other, way, part, w), ref, ref, to_vir=vir_at(w))

    def on_mir(way, part):
        ref = piece(0, False, way, part)
        arrived(("mir", way, part), ref)
        send(("zl", way, part), ref, ref, to_vir=vir_at(0, True))
        to_x(0, way, part)

    def on_zl(way, part):
        arrived(("zl", way, part), piece(0, True, way, part))
        to_x(1, way, part)

    def on_x(other, way, part, w):
        ref = piece(-w, other, way, part)
        arrived(("x", other, way, part, w), ref)
        if w == way:
            send(("xf", other, way, part), ref, ref, to_vir=vir_at(w))

    def on_xf(other, way, part):
        arrived(("xf", other, way, part), piece(2, other, way, part))

    odd = y % 2
    needs = ((0, 1, -1), (2, -2), (3, -3), (4,))

    def tiles_of(k):
        group = (y // 2 + jnp.where(odd == 1, (0, 1, -1, 2)[k], (0, -1, 1, 2)[k]) + 4) % 4
        return [4 * t + group for t in range(3)]

    def product(k, left):
        lanes = [pl.ds(pl.multiple_of(128 * t, 128), 128) for t in tiles_of(k)]
        right = jnp.concatenate([packed[:, :, :, n].reshape(1024, 128) for n in lanes], axis=1)
        zero = jnp.concatenate([zeros[t] for t in tiles_of(k)], axis=1) == 1
        a = jnp.dot(left(slice(0, 1024)), right, preferred_element_type=jnp.float32)
        b = jnp.dot(left(slice(1024, 2048)), right, preferred_element_type=jnp.float32)
        return jnp.where(zero, a, b)

    def on_inverse():
        @pl.loop(0, 12)
        def _(t):
            inverse[t] = 1.0 / (vir_energy[pl.ds(t, 1), :] - occ_column[...])

    def on_own(k):
        for delta in needs[k]:
            for s in range(4):
                arrived(("sib", delta, s), slot(delta, s, sibling=True), when=valid(s))
        total[k] = product(k, lambda lanes: own[:, lanes])

    def on_mirror(k):
        value = total[k] - product(k, lambda lanes: mirrored[:, :, :, lanes].reshape(512, 1024))
        for n, t in enumerate(tiles_of(k)):
            columns = pl.ds(pl.multiple_of(128 * t, 128), 128)
            out[:, columns] = (value[:, 128 * n : 128 * n + 128] * inverse[t]).astype(jnp.bfloat16)

    def sort_rows(chunk):
        rows = pl.ds(pl.multiple_of(64 * chunk, 64), 64)
        low = lax.broadcasted_iota(jnp.int32, (64, 128), 1) < TILE

        def tile(p, half):
            value = plain[order[8, p], chunk].astype(jnp.float32)
            there = jnp.broadcast_to(order[16, p], (64, 128)) == half
            return jnp.where(there, value, pltpu.roll(value, TILE, 1))

        for b in range(16):
            pair = jnp.where(low, tile(2 * b, 0), tile(2 * b + 1, 1))
            own[rows, 128 * b : 128 * b + 128] = pair.astype(jnp.bfloat16)

    def on_sort():
        @pl.loop(1, 8)
        def _(i):
            sort_rows((vir + i) % 8)

    def local(source, target, k):
        copy = pltpu.make_async_copy(source, target, local_sems.at[k])
        copy.start()
        return copy

    labels_copies = [local(row_labels_hbm, row_labels, 0), local(column_labels_hbm, column_labels, 1)]
    plain_copies = [local(amplitudes.at[:, :, pl.ds(128 * b, 128)], plain.at[b], 8 + b) for b in range(16)]
    energy_copies = [local(occ_energy_hbm, occ_energy, 3), local(vir_energy_hbm, vir_energy, 4)]

    @pl.when(owner)
    def _():
        pltpu.make_async_copy(integrals.at[:, columns_of(zh)], first.at[zh], local_sems.at[6]).start()

    barrier = pltpu.get_barrier_semaphore()
    peers = [(at(dy=d), vir) for d in (1, -1, 2, -2, 3, -3, 4)] + [(at(dz=d), vir) for d in (1, -1, 2)]
    peers += [(at(sibling=True), vir), (occ, vir_at(0, True)), (occ, vir_at(1)), (occ, vir_at(-1))]
    for peer in peers:
        pl.semaphore_signal(barrier, inc=1, device_id=peer, device_id_type=MESH)

    for copy in labels_copies:
        copy.wait()
    lane = lax.broadcasted_iota(jnp.int32, (8, 128), 1)
    places = [jnp.zeros((8, 128), jnp.int32)] * 3
    ones = jnp.int32(0)
    for r in range(32):
        label = row_labels[r]
        rank = jnp.minimum(jnp.where(label == 1, ones, r - ones), 15)
        here = lane == label * 16 + rank
        places = [jnp.where(here, n, place) for n, place in zip((r, r // 2, r % 2), places)]
        ones = ones + label
    for n in range(3):
        order_vmem[8 * n : 8 * n + 8, :] = places[n]
    order_copy = local(order_vmem, order, 2)

    pl.semaphore_wait(barrier, len(peers))
    send_first()

    for copy in plain_copies:
        copy.wait()
    order_copy.wait()
    sort_rows(vir)
    for way in (1, -1):
        send_mirror(way, 0)

    side = lax.broadcasted_iota(jnp.int32, (1, 128), 1) < TILE
    for t in range(12):
        zeros[t] = jnp.where(jnp.where(side, column_labels[2 * t], column_labels[2 * t + 1]) == 0, 1, 0)
    for copy in energy_copies:
        copy.wait()
    for b in range(4):
        occ_column[128 * b : 128 * b + 128, :] = jnp.transpose(
            jnp.broadcast_to(occ_energy[b : b + 1, :], (128, 128))
        )

    handlers = {
        "a1": on_first, "a2": on_second, "z": on_z, "y": on_y, "zf": on_zf, "relay": on_relay, "mir": on_mir,
        "zl": on_zl, "x": on_x, "xf": on_xf, "sort": on_sort, "inverse": on_inverse, "own": on_own,
        "mirror": on_mirror,
    }
    for kind, *place in ORDER:
        handlers[kind](*place)
    for wait in pending:
        wait()


def body(amplitudes, integrals, row_irreps, column_irreps, occ_energy, vir_energy):
    hbm = pl.BlockSpec(memory_space=pltpu.HBM)
    return pl.pallas_call(
        kernel,
        out_shape=pltpu.VMEM((512, 1536), jnp.bfloat16),
        in_specs=[hbm] * 6,
        out_specs=pl.BlockSpec(memory_space=pltpu.VMEM),
        scratch_shapes=[
            pltpu.VMEM((16, 4, 16, 1536), jnp.bfloat16),
            pltpu.VMEM((8, 4, 16, 2048), jnp.bfloat16),
            pltpu.VMEM((16, 8, 64, 128), jnp.bfloat16),
            pltpu.VMEM((512, 2048), jnp.bfloat16),
            pltpu.VMEM((4, 512, 384), jnp.float32),
            pltpu.VMEM((12, 512, 128), jnp.float32),
            pltpu.VMEM((4, 32, 512), jnp.bfloat16),
            pltpu.VMEM((32, 16, 128), jnp.bfloat16),
            pltpu.VMEM((4, 16, 2048), jnp.bfloat16),
            pltpu.VMEM((4, 128), jnp.float32),
            pltpu.VMEM((12, 128), jnp.float32),
            pltpu.VMEM((512, 128), jnp.float32),
            pltpu.VMEM((12, 1, 128), jnp.int32),
            pltpu.VMEM((24, 128), jnp.int32),
            pltpu.SMEM((24, 128), jnp.int32),
            pltpu.SMEM((32,), jnp.int32),
            pltpu.SMEM((24,), jnp.int32),
            pltpu.SemaphoreType.DMA((N_SEMS,)),
            pltpu.SemaphoreType.DMA((N_SEMS,)),
            pltpu.SemaphoreType.DMA((24,)),
        ],
        compiler_params=pltpu.CompilerParams(
            collective_id=0, has_side_effects=True, vmem_limit_bytes=58 * 2**20
        ),
        cost_estimate=pl.CostEstimate(flops=6442450944, bytes_accessed=4 * 2**20, transcendentals=0),
    )(
        row_irreps, column_irreps, integrals, amplitudes.reshape(8, 64, 2048),
        occ_energy.reshape(4, 128), vir_energy.reshape(12, 128),
    )


def solution(mesh):
    placed = (P("occ", None), P("occ", "vir"), P(), P("vir"), P("occ"), P("vir"))
    return jax.shard_map(
        body, mesh=mesh, in_specs=placed, out_specs=P("occ", "vir"), check_vma=False
    )
```

```python
import jax
import jax.numpy as jnp
from jax import lax
from jax.experimental import pallas as pl
from jax.experimental.pallas import tpu as pltpu
from jax.sharding import PartitionSpec as P

TILE = 64
MESH = pl.DeviceIdType.MESH
NY, NZ, NX = 8, 4, 4
DELTAS = (0, 1, -1, 2, -2, 3, -3, 4)
N_SEMS = 128
ORDER = (
    ("a1",), ("sort",), ("relay", 1, 0), ("relay", -1, 0), ("relay", 1, 1), ("relay", -1, 1), ("a2",), ("inverse",),
    ("mir", 1, 0), ("mir", -1, 0), ("z", 3), ("z", 1), ("mir", 1, 1), ("mir", -1, 1), ("x", 0, 1, 0, 1),
    ("x", 0, 1, 0, -1), ("zl", 1, 0), ("y", 0, 1, 1), ("y", 0, 1, -1), ("x", 0, -1, 0, 1),
    ("x", 0, -1, 0, -1), ("zl", -1, 0), ("y", 3, 1, 1), ("y", 3, 1, -1), ("zf",), ("y", 1, 1, 1),
    ("y", 1, 1, -1), ("x", 0, 1, 1, 1), ("x", 0, 1, 1, -1), ("y", 0, 2, 1), ("y", 0, 2, -1), ("zl", 1, 1),
    ("x", 0, -1, 1, 1), ("x", 0, -1, 1, -1), ("y", 3, 2, 1), ("y", 3, 2, -1), ("zl", -1, 1),
    ("xf", 0, 1, 0), ("xf", 0, -1, 0), ("y", 2, 1, 1), ("y", 2, 1, -1), ("x", 1, 1, 0, 1), ("y", 1, 2, 1),
    ("y", 1, 2, -1), ("xf", 0, 1, 1), ("x", 1, 1, 1, -1), ("y", 0, 3, 1), ("y", 0, 3, -1), ("own", 0),
    ("x", 1, 1, 0, -1), ("x", 1, 1, 1, 1), ("y", 3, 3, 1), ("xf", 0, -1, 1), ("y", 3, 3, -1),
    ("x", 1, -1, 0, 1), ("x", 1, -1, 1, 1), ("y", 2, 2, 1), ("y", 2, 2, -1), ("x", 1, -1, 1, -1),
    ("x", 1, -1, 0, -1), ("y", 1, 3, 1), ("y", 1, 3, -1), ("y", 0, 4), ("y", 3, 4), ("own", 1),
    ("xf", 1, 1, 0), ("xf", 1, 1, 1), ("y", 2, 3, 1), ("y", 2, 3, -1), ("y", 1, 4), ("xf", 1, -1, 0),
    ("xf", 1, -1, 1), ("mirror", 0), ("mirror", 1), ("y", 2, 4), ("own", 2), ("mirror", 2), ("own", 3),
    ("mirror", 3),
)


def kernel(
    row_labels_hbm, column_labels_hbm, integrals, amplitudes, occ_energy_hbm, vir_energy_hbm, out,
    packed, mirrored, plain, own, total, inverse, first, second, relay, landed_0, landed_1, landed_2, landed_3, occ_energy, vir_energy, occ_column, zeros,
    order_vmem, order, row_labels, column_labels, send_sems, recv_sems, local_sems,
):
    landed = (landed_0, landed_1, landed_2, landed_3)
    occ, vir = lax.axis_index("occ"), lax.axis_index("vir")
    core = occ % 2
    zh = (occ // 2) % NZ
    y = occ // (2 * NZ)
    zl = vir % 2
    x = vir // 2
    owner = zh != 3

    def at(dy=0, dz=0, sibling=False):
        c = 1 - core if sibling else core
        return (((y + dy + NY) % NY) * NZ + (zh + dz + NZ) % NZ) * 2 + c

    def vir_at(dx=0, other=False):
        return ((x + dx + NX) % NX) * 2 + (1 - zl if other else zl)

    def valid(stream):
        return (zh + stream) % NZ != 3

    names = {}
    pending = []

    def sem_of(name):
        return names.setdefault(name, len(names))

    def send(name, source, target, to_occ=None, to_vir=None, when=None):
        k = sem_of(name)

        def descriptor():
            return pltpu.make_async_remote_copy(
                src_ref=source(), dst_ref=target(), send_sem=send_sems.at[k], recv_sem=recv_sems.at[k],
                device_id=(occ if to_occ is None else to_occ, vir if to_vir is None else to_vir),
                device_id_type=MESH,
            )

        if when is None:
            descriptor().start()
            pending.append(lambda: descriptor().wait_send())
        else:
            pl.when(when)(lambda: descriptor().start())
            pending.append(lambda: pl.when(when)(lambda: descriptor().wait_send()))

    def arrived(name, target, when=None):
        k = sem_of(name)

        def wait():
            pltpu.make_async_remote_copy(
                src_ref=target(), dst_ref=target(), send_sem=send_sems.at[k], recv_sem=recv_sems.at[k],
                device_id=(at(sibling=True), vir), device_id_type=MESH,
            ).wait_recv()

        if when is None:
            wait()
        else:
            pl.when(when)(wait)

    def columns_of(t):
        return pl.ds(pl.multiple_of(512 * t, 512), 512)

    def send_first():
        for s in (1, 3, 2):
            t = (zh + s) % NZ
            send(("first", s), lambda t=t: integrals.at[:, columns_of(t)], lambda: first.at[zh], at(dz=s), when=t != 3)

    def unit(plane):
        rows = pl.ds(pl.multiple_of(16 * (plane % 2), 16), 16)
        return first.at[:, rows, pl.ds(pl.multiple_of(128 * (plane // 2), 128), 128)]

    def second_from(plane):
        return second.at[pl.ds(pl.multiple_of(4 * plane, 4), 4)]

    def on_first():
        for s in (1, 3, 2):
            arrived(("first", s), lambda s=s: first.at[(zh - s + NZ) % NZ], when=owner)

        @pl.when(owner)
        def _():
            pltpu.make_async_copy(integrals.at[:, columns_of(zh)], first.at[zh], local_sems.at[6]).wait()
            pltpu.make_async_copy(unit(y), second_from(y), local_sems.at[7]).start()

        for d in (4, 3, -3, 2, -2, 1, -1):
            plane = (y + d + NY) % NY
            send(("second", d), lambda p=plane: unit(p), lambda: second_from(y), at(dy=d), when=owner)

    def on_second():
        for d in (1, -1, 2, -2, 3, -3, 4):
            arrived(("second", d), lambda d=d: second_from((y - d + NY) % NY), when=owner)

        @pl.when(owner)
        def _():
            pltpu.make_async_copy(unit(y), second_from(y), local_sems.at[7]).wait()
            zero = jnp.broadcast_to(zeros[4 * zh + y // 2], (16, 128)) == 1
            columns = pl.ds(pl.multiple_of(128 * (4 * zh + y // 2), 128), 128)

            @pl.loop(0, 16)
            def _(p):
                a = second[order[0, p]].astype(jnp.float32)
                b = second[order[0, 16 + p]].astype(jnp.float32)
                packed[p, 2 * core + y % 2, :, columns] = jnp.where(zero, a, b).astype(jnp.bfloat16)

        for s in (3, 1):
            send(("z", s), slot(0, 0), slot(0, 0), at(dz=-s), when=owner)
        start_stream(0)

    def slot(delta, stream, half=None, sibling=False):
        def ref():
            plane, block = (y + delta + NY) % NY, (zh + stream) % NZ
            rows = slice(None) if half is None else pl.ds(8 * half, 8)
            columns = pl.ds(pl.multiple_of(128 * (4 * block + plane // 2), 128), 128)
            c = 1 - core if sibling else core
            return packed.at[rows, 2 * c + plane % 2, :, columns]

        return ref

    def half_of(distance, way):
        return None if distance < 4 else (0 if way > 0 else 1)

    def delta_of(distance, way):
        return 4 if distance == 4 else -way * distance

    def send_y(stream, distance, way):
        half = half_of(distance, way)
        ref = slot(delta_of(distance - 1, way), stream, half)
        send(("y", stream, distance, way), ref, ref, at(dy=way), when=valid(stream))

    def to_sibling(delta, stream):
        ref = slot(delta, stream)
        send(("sib", delta, stream), ref, ref, at(sibling=True), when=valid(stream))

    def start_stream(stream):
        send_y(stream, 1, 1)
        send_y(stream, 1, -1)
        to_sibling(0, stream)

    def on_z(stream):
        arrived(("z", stream), slot(0, stream), when=valid(stream))
        way = 1 if stream == 3 else -1
        half = 0 if way > 0 else 1
        ref = slot(0, stream, half)
        send(("zf", half), ref, ref, at(dz=way), when=valid(stream))
        start_stream(stream)

    def on_zf():
        for half in (0, 1):
            arrived(("zf", half), slot(0, 2, half), when=valid(2))
        start_stream(2)

    def on_y(stream, distance, way=None):
        for w in (1, -1) if way is None else (way,):
            ref = slot(delta_of(distance, w), stream, half_of(distance, w))
            arrived(("y", stream, distance, w), ref, when=valid(stream))
        if distance < 4:
            send_y(stream, distance + 1, way)
        to_sibling(delta_of(distance, way), stream)

    def index_of(way, part):
        return part + (0 if way > 0 else 2)

    def piece(dx, other, way, part):
        return lambda: mirrored.at[vir_at(dx, other), index_of(way, part)]

    def relay_of(way, part):
        return lambda: relay.at[index_of(way, part)]

    def landed_of(way, part):
        return lambda: landed[index_of(way, part)]

    def send_mirror(way, part):
        rows = pl.ds(16 * index_of(way, part), 16)
        send(("relay", way, part), lambda: plain.at[:, vir, rows], relay_of(way, part), at(dy=2 * way))

    def on_relay(way, part):
        arrived(("relay", way, part), relay_of(way, part))
        send(("mir", way, part), relay_of(way, part), landed_of(way, part), at(dy=2 * way))

    def to_x(other, way, part):
        ref = piece(0, other, way, part)
        for w in (1, -1):
            send(("x", other, way, part, w), ref, ref, to_vir=vir_at(w))

    def to_other(name, ref):
        send(name, ref, ref, to_vir=vir_at(0, True))

    def on_mir(way, part):
        arrived(("mir", way, part), landed_of(way, part))
        n = index_of(way, part)
        for b in range(16):
            mirrored[vir, n, :, 128 * b : 128 * b + 128] = sorted_block(lambda i: landed[n][i], b, 16)
        if part == 0:
            to_x(0, way, part)
            to_other(("zl", way, part), piece(0, False, way, part))
        else:
            to_other(("zl", way, part), piece(0, False, way, part))
            to_x(0, way, part)

    def on_zl(way, part):
        arrived(("zl", way, part), piece(0, True, way, part))
        if part == 1:
            to_x(1, way, part)

    def on_x(other, way, part, w):
        if other and part == 0:
            arrived(("x", 1, way, part, w), piece(-w, True, way, part))
            return
        ref = piece(-w, other, way, part)
        arrived(("x", other, way, part, w), ref)
        if w == way:
            send(("xf", other, way, part), ref, ref, to_vir=vir_at(w))
        if part == 0:
            to_other(("x", 1, way, part, w), ref)

    def on_xf(other, way, part):
        ref = piece(2, other, way, part)
        arrived(("xf", other, way, part), ref)
        if part == 0 and not other:
            to_other(("xf", 1, way, part), ref)

    odd = y % 2
    needs = ((0, 1, -1), (2, -2), (3, -3), (4,))

    def tiles_of(k):
        group = (y // 2 + jnp.where(odd == 1, (0, 1, -1, 2)[k], (0, -1, 1, 2)[k]) + 4) % 4
        return [4 * t + group for t in range(3)]

    def product(k, left):
        lanes = [pl.ds(pl.multiple_of(128 * t, 128), 128) for t in tiles_of(k)]
        right = jnp.concatenate([packed[:, :, :, n].reshape(1024, 128) for n in lanes], axis=1)
        zero = jnp.concatenate([zeros[t] for t in tiles_of(k)], axis=1) == 1
        a = jnp.dot(left(slice(0, 1024)), right, preferred_element_type=jnp.float32)
        b = jnp.dot(left(slice(1024, 2048)), right, preferred_element_type=jnp.float32)
        return jnp.where(zero, a, b)

    def on_inverse():
        @pl.loop(0, 12)
        def _(t):
            inverse[t] = 1.0 / (vir_energy[pl.ds(t, 1), :] - occ_column[...])

    def on_own(k):
        for delta in needs[k]:
            for s in range(4):
                arrived(("sib", delta, s), slot(delta, s, sibling=True), when=valid(s))
        total[k] = product(k, lambda lanes: own[:, lanes])

    def on_mirror(k):
        value = total[k] - product(k, lambda lanes: mirrored[:, :, :, lanes].reshape(512, 1024))
        for n, t in enumerate(tiles_of(k)):
            columns = pl.ds(pl.multiple_of(128 * t, 128), 128)
            out[:, columns] = (value[:, 128 * n : 128 * n + 128] * inverse[t]).astype(jnp.bfloat16)

    def sorted_block(block, b, rows):
        low = lax.broadcasted_iota(jnp.int32, (rows, 128), 1) < TILE

        def tile(p, half):
            value = block(order[8, p]).astype(jnp.float32)
            there = jnp.broadcast_to(order[16, p], (rows, 128)) == half
            return jnp.where(there, value, pltpu.roll(value, TILE, 1))

        return jnp.where(low, tile(2 * b, 0), tile(2 * b + 1, 1)).astype(jnp.bfloat16)

    def on_sort():
        @pl.loop(0, 8)
        def _(chunk):
            rows = pl.ds(pl.multiple_of(64 * chunk, 64), 64)
            for b in range(16):
                own[rows, 128 * b : 128 * b + 128] = sorted_block(lambda i: plain[i, chunk], b, 64)

    def local(source, target, k):
        copy = pltpu.make_async_copy(source, target, local_sems.at[k])
        copy.start()
        return copy

    labels_copies = [local(row_labels_hbm, row_labels, 0), local(column_labels_hbm, column_labels, 1)]
    plain_copies = [local(amplitudes.at[:, :, pl.ds(128 * b, 128)], plain.at[b], 8 + b) for b in range(16)]
    energy_copies = [local(occ_energy_hbm, occ_energy, 3), local(vir_energy_hbm, vir_energy, 4)]

    @pl.when(owner)
    def _():
        pltpu.make_async_copy(integrals.at[:, columns_of(zh)], first.at[zh], local_sems.at[6]).start()

    barrier = pltpu.get_barrier_semaphore()
    peers = [(at(dy=d), vir) for d in (1, -1, 2, -2, 3, -3, 4)] + [(at(dz=d), vir) for d in (1, -1, 2)]
    peers += [(at(sibling=True), vir), (occ, vir_at(0, True)), (occ, vir_at(1)), (occ, vir_at(-1))]
    for peer in peers:
        pl.semaphore_signal(barrier, inc=1, device_id=peer, device_id_type=MESH)

    pl.semaphore_wait(barrier, len(peers))
    send_first()
    for copy in plain_copies:
        copy.wait()
    for part in (0, 1):
        for way in (1, -1):
            send_mirror(way, part)

    for copy in labels_copies:
        copy.wait()
    lane = lax.broadcasted_iota(jnp.int32, (8, 128), 1)
    places = [jnp.zeros((8, 128), jnp.int32)] * 3
    ones = jnp.int32(0)
    for r in range(32):
        label = row_labels[r]
        rank = jnp.minimum(jnp.where(label == 1, ones, r - ones), 15)
        here = lane == label * 16 + rank
        places = [jnp.where(here, n, place) for n, place in zip((r, r // 2, r % 2), places)]
        ones = ones + label
    for n in range(3):
        order_vmem[8 * n : 8 * n + 8, :] = places[n]
    order_copy = local(order_vmem, order, 2)

    side = lax.broadcasted_iota(jnp.int32, (1, 128), 1) < TILE
    for t in range(12):
        zeros[t] = jnp.where(jnp.where(side, column_labels[2 * t], column_labels[2 * t + 1]) == 0, 1, 0)
    for copy in energy_copies:
        copy.wait()
    for b in range(4):
        occ_column[128 * b : 128 * b + 128, :] = jnp.transpose(
            jnp.broadcast_to(occ_energy[b : b + 1, :], (128, 128))
        )
    order_copy.wait()

    handlers = {
        "a1": on_first, "a2": on_second, "z": on_z, "y": on_y, "zf": on_zf, "relay": on_relay, "mir": on_mir,
        "zl": on_zl, "x": on_x, "xf": on_xf, "sort": on_sort, "inverse": on_inverse, "own": on_own,
        "mirror": on_mirror,
    }
    for kind, *place in ORDER:
        handlers[kind](*place)
    for wait in pending:
        wait()


def body(amplitudes, integrals, row_irreps, column_irreps, occ_energy, vir_energy):
    hbm = pl.BlockSpec(memory_space=pltpu.HBM)
    return pl.pallas_call(
        kernel,
        out_shape=pltpu.VMEM((512, 1536), jnp.bfloat16),
        in_specs=[hbm] * 6,
        out_specs=pl.BlockSpec(memory_space=pltpu.VMEM),
        scratch_shapes=[
            pltpu.VMEM((16, 4, 16, 1536), jnp.bfloat16),
            pltpu.VMEM((8, 4, 16, 2048), jnp.bfloat16),
            pltpu.VMEM((16, 8, 64, 128), jnp.bfloat16),
            pltpu.VMEM((512, 2048), jnp.bfloat16),
            pltpu.VMEM((4, 512, 384), jnp.float32),
            pltpu.VMEM((12, 512, 128), jnp.float32),
            pltpu.VMEM((4, 32, 512), jnp.bfloat16),
            pltpu.VMEM((32, 16, 128), jnp.bfloat16),
            pltpu.VMEM((4, 16, 16, 128), jnp.bfloat16),
            *[pltpu.VMEM((16, 16, 128), jnp.bfloat16)] * 4,
            pltpu.VMEM((4, 128), jnp.float32),
            pltpu.VMEM((12, 128), jnp.float32),
            pltpu.VMEM((512, 128), jnp.float32),
            pltpu.VMEM((12, 1, 128), jnp.int32),
            pltpu.VMEM((24, 128), jnp.int32),
            pltpu.SMEM((24, 128), jnp.int32),
            pltpu.SMEM((32,), jnp.int32),
            pltpu.SMEM((24,), jnp.int32),
            pltpu.SemaphoreType.DMA((N_SEMS,)),
            pltpu.SemaphoreType.DMA((N_SEMS,)),
            pltpu.SemaphoreType.DMA((24,)),
        ],
        compiler_params=pltpu.CompilerParams(
            collective_id=0, has_side_effects=True, vmem_limit_bytes=58 * 2**20
        ),
        cost_estimate=pl.CostEstimate(flops=6442450944, bytes_accessed=4 * 2**20, transcendentals=0),
    )(
        row_irreps, column_irreps, integrals, amplitudes.reshape(8, 64, 2048),
        occ_energy.reshape(4, 128), vir_energy.reshape(12, 128),
    )


def solution(mesh):
    placed = (P("occ", None), P("occ", "vir"), P(), P("vir"), P("occ"), P("vir"))
    return jax.shard_map(
        body, mesh=mesh, in_specs=placed, out_specs=P("occ", "vir"), check_vma=False
    )
```

```python
import jax
import jax.numpy as jnp
from jax import lax
from jax.experimental import pallas as pl
from jax.experimental.pallas import tpu as pltpu
from jax.sharding import PartitionSpec as P

TILE = 64
MESH = pl.DeviceIdType.MESH
NY, NZ, NX = 8, 4, 4
DELTAS = (0, 1, -1, 2, -2, 3, -3, 4)
N_SEMS = 128
ORDER = (
    ("a1",), ("sort",), ("relay", 1, 0), ("relay", 1, 1), ("relay", -1, 0), ("relay", -1, 1), ("a2",), ("inverse",),
    ("mir", 1, 0), ("mir", -1, 0), ("z", 3), ("mir", 1, 1), ("z", 1), ("mir", -1, 1), ("y", 0, 1, 1),
    ("y", 0, 1, -1), ("z", 2), ("x", 0, -1, 0, -1), ("y", 3, 1, -1), ("x", 0, 1, 0, 1), ("x", 0, -1, 0, 1),
    ("y", 3, 1, 1), ("y", 1, 1, 1), ("y", 1, 1, -1), ("y", 0, 2, 1), ("y", 0, 2, -1), ("x", 0, 1, 0, -1),
    ("zl", 1, 1), ("y", 2, 1, 1), ("zl", -1, 0), ("y", 2, 1, -1), ("x", 0, -1, 1, 1), ("zl", -1, 1),
    ("zl", 1, 0), ("x", 0, 1, 1, -1), ("xf", 0, -1, 0), ("x", 0, -1, 1, -1), ("y", 3, 2, 1),
    ("y", 3, 2, -1), ("xf", 0, 1, 0), ("y", 1, 2, -1), ("y", 1, 2, 1), ("y", 0, 3, 1), ("y", 0, 3, -1),
    ("own", 0, 0), ("y", 2, 2, 1), ("x", 1, 1, 1, -1), ("y", 2, 2, -1), ("x", 1, 1, 1, 1), ("own", 3, 0),
    ("y", 3, 3, -1), ("y", 3, 3, 1), ("x", 0, 1, 1, 1), ("x", 1, -1, 1, -1), ("y", 1, 3, 1),
    ("y", 1, 3, -1), ("y", 0, 4), ("x", 1, -1, 0, -1), ("own", 1, 0), ("y", 2, 3, -1), ("y", 2, 3, 1),
    ("x", 1, -1, 1, 1), ("x", 1, 1, 0, 1), ("y", 3, 4), ("xf", 1, -1, 0), ("xf", 0, -1, 1), ("own", 2, 0),
    ("y", 1, 4), ("own", 0, 1), ("xf", 1, -1, 1), ("xf", 0, 1, 1), ("x", 1, -1, 0, 1), ("x", 1, 1, 0, -1),
    ("xf", 1, 1, 0), ("xf", 1, 1, 1), ("mirror", 0, 1), ("mirror", 1, 0), ("mirror", 0, 0), ("y", 2, 4),
    ("mirror", 3, 0), ("own", 3, 1), ("own", 1, 1), ("mirror", 3, 1), ("mirror", 1, 1), ("mirror", 2, 0),
    ("own", 2, 1), ("mirror", 2, 1),
)


def kernel(
    row_labels_hbm, column_labels_hbm, integrals, amplitudes, occ_energy_hbm, vir_energy_hbm, out,
    packed, mirrored, plain, own, total, inverse, first, second, relay, landed_0, landed_1, landed_2, landed_3, occ_energy, vir_energy, occ_column, zeros,
    order_vmem, order, row_labels, column_labels, send_sems, recv_sems, local_sems,
):
    landed = (landed_0, landed_1, landed_2, landed_3)
    occ, vir = lax.axis_index("occ"), lax.axis_index("vir")
    core = occ % 2
    zh = (occ // 2) % NZ
    y = occ // (2 * NZ)
    zl = vir % 2
    x = vir // 2
    owner = zh != 3

    def at(dy=0, dz=0, sibling=False):
        c = 1 - core if sibling else core
        return (((y + dy + NY) % NY) * NZ + (zh + dz + NZ) % NZ) * 2 + c

    def vir_at(dx=0, other=False):
        return ((x + dx + NX) % NX) * 2 + (1 - zl if other else zl)

    def valid(stream):
        return (zh + stream) % NZ != 3

    names = {}
    pending = []

    def sem_of(name):
        return names.setdefault(name, len(names))

    def send(name, source, target, to_occ=None, to_vir=None, when=None):
        k = sem_of(name)

        def descriptor():
            return pltpu.make_async_remote_copy(
                src_ref=source(), dst_ref=target(), send_sem=send_sems.at[k], recv_sem=recv_sems.at[k],
                device_id=(occ if to_occ is None else to_occ, vir if to_vir is None else to_vir),
                device_id_type=MESH,
            )

        if when is None:
            descriptor().start()
            pending.append(lambda: descriptor().wait_send())
        else:
            pl.when(when)(lambda: descriptor().start())
            pending.append(lambda: pl.when(when)(lambda: descriptor().wait_send()))

    def arrived(name, target, when=None):
        k = sem_of(name)

        def wait():
            pltpu.make_async_remote_copy(
                src_ref=target(), dst_ref=target(), send_sem=send_sems.at[k], recv_sem=recv_sems.at[k],
                device_id=(at(sibling=True), vir), device_id_type=MESH,
            ).wait_recv()

        if when is None:
            wait()
        else:
            pl.when(when)(wait)

    def columns_of(t):
        return pl.ds(pl.multiple_of(512 * t, 512), 512)

    def send_first():
        for s in (1, 3, 2):
            t = (zh + s) % NZ
            send(("first", s), lambda t=t: integrals.at[:, columns_of(t)], lambda: first.at[zh], at(dz=s), when=t != 3)

    def unit(plane):
        rows = pl.ds(pl.multiple_of(16 * (plane % 2), 16), 16)
        return first.at[:, rows, pl.ds(pl.multiple_of(128 * (plane // 2), 128), 128)]

    def second_from(plane):
        return second.at[pl.ds(pl.multiple_of(4 * plane, 4), 4)]

    def on_first():
        for s in (1, 3, 2):
            arrived(("first", s), lambda s=s: first.at[(zh - s + NZ) % NZ], when=owner)

        @pl.when(owner)
        def _():
            pltpu.make_async_copy(integrals.at[:, columns_of(zh)], first.at[zh], local_sems.at[6]).wait()
            pltpu.make_async_copy(unit(y), second_from(y), local_sems.at[7]).start()

        for d in (4, 3, -3, 2, -2, 1, -1):
            plane = (y + d + NY) % NY
            send(("second", d), lambda p=plane: unit(p), lambda: second_from(y), at(dy=d), when=owner)

    def on_second():
        for d in (1, -1, 2, -2, 3, -3, 4):
            arrived(("second", d), lambda d=d: second_from((y - d + NY) % NY), when=owner)

        @pl.when(owner)
        def _():
            pltpu.make_async_copy(unit(y), second_from(y), local_sems.at[7]).wait()
            zero = jnp.broadcast_to(zeros[4 * zh + y // 2], (16, 128)) == 1
            columns = pl.ds(pl.multiple_of(128 * (4 * zh + y // 2), 128), 128)

            @pl.loop(0, 16)
            def _(p):
                a = second[order[0, p]].astype(jnp.float32)
                b = second[order[0, 16 + p]].astype(jnp.float32)
                packed[p, 2 * core + y % 2, :, columns] = jnp.where(zero, a, b).astype(jnp.bfloat16)

        for s in (3, 1):
            send(("z", s), slot(0, 0), slot(0, 0), at(dz=-s), when=owner)
        start_stream(0)
        send(("z", 2), slot(0, 0), slot(0, 0), at(dz=2), when=owner)

    def slot(delta, stream, half=None, sibling=False):
        def ref():
            plane, block = (y + delta + NY) % NY, (zh + stream) % NZ
            rows = slice(None) if half is None else pl.ds(8 * half, 8)
            columns = pl.ds(pl.multiple_of(128 * (4 * block + plane // 2), 128), 128)
            c = 1 - core if sibling else core
            return packed.at[rows, 2 * c + plane % 2, :, columns]

        return ref

    def half_of(distance, way):
        return None if distance < 4 else (0 if way > 0 else 1)

    def delta_of(distance, way):
        return 4 if distance == 4 else -way * distance

    def send_y(stream, distance, way):
        half = half_of(distance, way)
        ref = slot(delta_of(distance - 1, way), stream, half)
        send(("y", stream, distance, way), ref, ref, at(dy=way), when=valid(stream))

    def to_sibling(delta, stream):
        ref = slot(delta, stream)
        send(("sib", delta, stream), ref, ref, at(sibling=True), when=valid(stream))

    def start_stream(stream):
        send_y(stream, 1, 1)
        send_y(stream, 1, -1)
        to_sibling(0, stream)

    def on_z(stream):
        arrived(("z", stream), slot(0, stream), when=valid(stream))
        start_stream(stream)

    def on_y(stream, distance, way=None):
        for w in (1, -1) if way is None else (way,):
            ref = slot(delta_of(distance, w), stream, half_of(distance, w))
            arrived(("y", stream, distance, w), ref, when=valid(stream))
        if distance < 4:
            send_y(stream, distance + 1, way)
        to_sibling(delta_of(distance, way), stream)

    def index_of(way, part):
        return part + (0 if way > 0 else 2)

    def piece(dx, other, way, part):
        return lambda: mirrored.at[vir_at(dx, other), index_of(way, part)]

    def relay_of(way, part):
        return lambda: relay.at[index_of(way, part)]

    def landed_of(way, part):
        return lambda: landed[index_of(way, part)]

    def send_mirror(way, part):
        rows = pl.ds(16 * index_of(way, part), 16)
        send(("relay", way, part), lambda: plain.at[:, vir, rows], relay_of(way, part), at(dy=2 * way))

    def on_relay(way, part):
        arrived(("relay", way, part), relay_of(way, part))
        send(("mir", way, part), relay_of(way, part), landed_of(way, part), at(dy=2 * way))

    def to_x(other, way, part):
        ref = piece(0, other, way, part)
        for w in (1, -1):
            send(("x", other, way, part, w), ref, ref, to_vir=vir_at(w))

    def to_other(name, ref):
        send(name, ref, ref, to_vir=vir_at(0, True))

    def on_mir(way, part):
        arrived(("mir", way, part), landed_of(way, part))
        n = index_of(way, part)

        @pl.loop(0, 16, unroll=8)
        def _(b):
            lanes = pl.ds(pl.multiple_of(128 * b, 128), 128)
            mirrored[vir, n, :, lanes] = sorted_block(lambda i: landed[n][i], b, 16)

        if part == 0:
            to_x(0, way, part)
            to_other(("zl", way, part), piece(0, False, way, part))
        else:
            to_other(("zl", way, part), piece(0, False, way, part))
            to_x(0, way, part)

    def on_zl(way, part):
        arrived(("zl", way, part), piece(0, True, way, part))
        if part == 1:
            to_x(1, way, part)

    def on_x(other, way, part, w):
        if other and part == 0:
            arrived(("x", 1, way, part, w), piece(-w, True, way, part))
            return
        ref = piece(-w, other, way, part)
        arrived(("x", other, way, part, w), ref)
        if w == way:
            send(("xf", other, way, part), ref, ref, to_vir=vir_at(w))
        if part == 0:
            to_other(("x", 1, way, part, w), ref)

    def on_xf(other, way, part):
        ref = piece(2, other, way, part)
        arrived(("xf", other, way, part), ref)
        if part == 0 and not other:
            to_other(("xf", 1, way, part), ref)

    odd = y % 2
    needs = ((0, 1, -1, 2, -2), (3, -3, 4))

    def tiles_of(stream, half):
        steps = (((0, 0), (-1, 1)), ((1, -1), (2, 2)))[half]
        block = (zh + stream) % NZ
        return [4 * block + (y // 2 + jnp.where(odd == 1, o, e) + 4) % 4 for e, o in steps]

    def product(tiles, left):
        lanes = [pl.ds(pl.multiple_of(128 * t, 128), 128) for t in tiles]
        right = jnp.concatenate([packed[:, :, :, n].reshape(1024, 128) for n in lanes], axis=1)
        zero = jnp.concatenate([zeros[t] for t in tiles], axis=1) == 1
        a = jnp.dot(left(slice(0, 1024)), right, preferred_element_type=jnp.float32)
        b = jnp.dot(left(slice(1024, 2048)), right, preferred_element_type=jnp.float32)
        return jnp.where(zero, a, b)

    def on_inverse():
        @pl.loop(0, 12)
        def _(t):
            inverse[t] = 1.0 / (vir_energy[pl.ds(t, 1), :] - occ_column[...])

    def on_own(stream, half):
        @pl.when(valid(stream))
        def _():
            for delta in needs[half]:
                arrived(("sib", delta, stream), slot(delta, stream, sibling=True))
            total[2 * stream + half] = product(tiles_of(stream, half), lambda lanes: own[:, lanes])

    def on_mirror(stream, half):
        @pl.when(valid(stream))
        def _():
            tiles = tiles_of(stream, half)
            value = total[2 * stream + half] - product(
                tiles, lambda lanes: mirrored[:, :, :, lanes].reshape(512, 1024)
            )
            for n, t in enumerate(tiles):
                columns = pl.ds(pl.multiple_of(128 * t, 128), 128)
                out[:, columns] = (value[:, 128 * n : 128 * n + 128] * inverse[t]).astype(jnp.bfloat16)

    def sorted_block(block, b, rows):
        low = lax.broadcasted_iota(jnp.int32, (rows, 128), 1) < TILE

        def tile(p, half):
            value = block(order[8, p]).astype(jnp.float32)
            there = jnp.broadcast_to(order[16, p], (rows, 128)) == half
            return jnp.where(there, value, pltpu.roll(value, TILE, 1))

        return jnp.where(low, tile(2 * b, 0), tile(2 * b + 1, 1)).astype(jnp.bfloat16)

    def on_sort():
        @pl.loop(0, 16)
        def _(b):
            lanes = pl.ds(pl.multiple_of(128 * b, 128), 128)
            own[:, lanes] = sorted_block(lambda i: plain[i].reshape(512, 128), b, 512)

    def local(source, target, k):
        copy = pltpu.make_async_copy(source, target, local_sems.at[k])
        copy.start()
        return copy

    labels_copies = [local(row_labels_hbm, row_labels, 0), local(column_labels_hbm, column_labels, 1)]
    plain_copies = [local(amplitudes.at[:, :, pl.ds(128 * b, 128)], plain.at[b], 8 + b) for b in range(16)]
    energy_copies = [local(occ_energy_hbm, occ_energy, 3), local(vir_energy_hbm, vir_energy, 4)]

    @pl.when(owner)
    def _():
        pltpu.make_async_copy(integrals.at[:, columns_of(zh)], first.at[zh], local_sems.at[6]).start()

    barrier = pltpu.get_barrier_semaphore()
    peers = [(at(dy=d), vir) for d in (1, -1, 2, -2, 3, -3, 4)] + [(at(dz=d), vir) for d in (1, -1, 2)]
    peers += [(at(sibling=True), vir), (occ, vir_at(0, True)), (occ, vir_at(1)), (occ, vir_at(-1))]
    for peer in peers:
        pl.semaphore_signal(barrier, inc=1, device_id=peer, device_id_type=MESH)

    pl.semaphore_wait(barrier, len(peers))
    send_first()
    for copy in plain_copies:
        copy.wait()
    for part in (0, 1):
        for way in (1, -1):
            send_mirror(way, part)

    for copy in labels_copies:
        copy.wait()
    lane = lax.broadcasted_iota(jnp.int32, (8, 128), 1)
    places = [jnp.zeros((8, 128), jnp.int32)] * 3
    ones = jnp.int32(0)
    for r in range(32):
        label = row_labels[r]
        rank = jnp.minimum(jnp.where(label == 1, ones, r - ones), 15)
        here = lane == label * 16 + rank
        places = [jnp.where(here, n, place) for n, place in zip((r, r // 2, r % 2), places)]
        ones = ones + label
    for n in range(3):
        order_vmem[8 * n : 8 * n + 8, :] = places[n]
    order_copy = local(order_vmem, order, 2)

    side = lax.broadcasted_iota(jnp.int32, (1, 128), 1) < TILE
    for t in range(12):
        zeros[t] = jnp.where(jnp.where(side, column_labels[2 * t], column_labels[2 * t + 1]) == 0, 1, 0)
    for copy in energy_copies:
        copy.wait()
    for b in range(4):
        occ_column[128 * b : 128 * b + 128, :] = jnp.transpose(
            jnp.broadcast_to(occ_energy[b : b + 1, :], (128, 128))
        )
    order_copy.wait()

    handlers = {
        "a1": on_first, "a2": on_second, "z": on_z, "y": on_y, "relay": on_relay, "mir": on_mir,
        "zl": on_zl, "x": on_x, "xf": on_xf, "sort": on_sort, "inverse": on_inverse, "own": on_own,
        "mirror": on_mirror,
    }
    for kind, *place in ORDER:
        handlers[kind](*place)
    for wait in pending:
        wait()


def body(amplitudes, integrals, row_irreps, column_irreps, occ_energy, vir_energy):
    hbm = pl.BlockSpec(memory_space=pltpu.HBM)
    return pl.pallas_call(
        kernel,
        out_shape=pltpu.VMEM((512, 1536), jnp.bfloat16),
        in_specs=[hbm] * 6,
        out_specs=pl.BlockSpec(memory_space=pltpu.VMEM),
        scratch_shapes=[
            pltpu.VMEM((16, 4, 16, 1536), jnp.bfloat16),
            pltpu.VMEM((8, 4, 16, 2048), jnp.bfloat16),
            pltpu.VMEM((16, 8, 64, 128), jnp.bfloat16),
            pltpu.VMEM((512, 2048), jnp.bfloat16),
            pltpu.VMEM((8, 512, 256), jnp.float32),
            pltpu.VMEM((12, 512, 128), jnp.float32),
            pltpu.VMEM((4, 32, 512), jnp.bfloat16),
            pltpu.VMEM((32, 16, 128), jnp.bfloat16),
            pltpu.VMEM((4, 16, 16, 128), jnp.bfloat16),
            *[pltpu.VMEM((16, 16, 128), jnp.bfloat16)] * 4,
            pltpu.VMEM((4, 128), jnp.float32),
            pltpu.VMEM((12, 128), jnp.float32),
            pltpu.VMEM((512, 128), jnp.float32),
            pltpu.VMEM((12, 1, 128), jnp.int32),
            pltpu.VMEM((24, 128), jnp.int32),
            pltpu.SMEM((24, 128), jnp.int32),
            pltpu.SMEM((32,), jnp.int32),
            pltpu.SMEM((24,), jnp.int32),
            pltpu.SemaphoreType.DMA((N_SEMS,)),
            pltpu.SemaphoreType.DMA((N_SEMS,)),
            pltpu.SemaphoreType.DMA((24,)),
        ],
        compiler_params=pltpu.CompilerParams(
            collective_id=0, has_side_effects=True, vmem_limit_bytes=58 * 2**20
        ),
        cost_estimate=pl.CostEstimate(flops=6442450944, bytes_accessed=4 * 2**20, transcendentals=0),
    )(
        row_irreps, column_irreps, integrals, amplitudes.reshape(8, 64, 2048),
        occ_energy.reshape(4, 128), vir_energy.reshape(12, 128),
    )


def solution(mesh):
    placed = (P("occ", None), P("occ", "vir"), P(), P("vir"), P("occ"), P("vir"))
    return jax.shard_map(
        body, mesh=mesh, in_specs=placed, out_specs=P("occ", "vir"), check_vma=False
    )
```

```python
import jax
import jax.numpy as jnp
from jax import lax
from jax.experimental import pallas as pl
from jax.experimental.pallas import tpu as pltpu
from jax.sharding import PartitionSpec as P

TILE = 64
MESH = pl.DeviceIdType.MESH
NY, NZ, NX = 8, 4, 4
DELTAS = (0, 1, -1, 2, -2, 3, -3, 4)
N_SEMS = 128
ORDER = (
    ("sort", 4), ("sort", 7), ("sort", 6), ("sort", 1), ("sort", 0), ("a1",), ("inverse", 3), ("relay", 1, 0),
    ("relay", -1, 0), ("relay", 1, 1), ("a2",), ("relay", -1, 1), ("mir", 1, 0),
    ("inverse", 1), ("inverse", 2), ("mir", -1, 0), ("sort", 3), ("z", 3), ("mir", 1, 1), ("z", 1),
    ("y", 0, 1, -1), ("flush", 30), ("y", 0, 1, 1), ("mir", -1, 1), ("x", 0, 1, 0, -1), ("z", 2),
    ("flush", 30), ("y", 3, 1, -1), ("x", 0, -1, 0, -1), ("y", 3, 1, 1), ("sort", 2), ("flush", 30),
    ("y", 1, 1, -1), ("y", 1, 1, 1), ("zl", -1, 0), ("x", 0, 1, 0, 1), ("y", 0, 2, 1), ("y", 0, 2, -1),
    ("zl", 1, 0), ("flush", 30), ("zl", 1, 1), ("x", 0, 1, 1, 1), ("inverse", 0), ("x", 0, -1, 1, 1),
    ("y", 2, 1, -1), ("y", 2, 1, 1), ("flush", 30), ("y", 3, 2, 1), ("zl", -1, 1), ("x", 0, 1, 1, -1),
    ("x", 0, -1, 1, -1), ("y", 3, 2, -1), ("flush", 30), ("y", 1, 2, -1), ("xf", 0, 1, 0), ("y", 1, 2, 1),
    ("y", 0, 3, 1), ("x", 0, -1, 0, 1), ("y", 0, 3, -1), ("sort", 5), ("flush", 30), ("y", 2, 2, 1),
    ("x", 1, 1, 1, 1), ("xf", 0, -1, 0), ("y", 2, 2, -1), ("own", 0, 0), ("own", 1, 0), ("y", 3, 3, 1),
    ("y", 3, 3, -1), ("x", 1, 1, 1, -1), ("x", 1, -1, 1, -1), ("flush", 30), ("y", 1, 3, 1),
    ("y", 1, 3, -1), ("x", 1, -1, 0, -1), ("y", 0, 4), ("own", 2, 0), ("x", 1, 1, 0, -1), ("xf", 1, 1, 0),
    ("flush", 30), ("y", 2, 3, 1), ("y", 2, 3, -1), ("xf", 0, 1, 1), ("xf", 0, -1, 1), ("x", 1, -1, 0, 1),
    ("y", 3, 4), ("own", 3, 0), ("xf", 1, 1, 1), ("y", 1, 4), ("own", 0, 1), ("x", 1, 1, 0, 1),
    ("xf", 1, -1, 1), ("xf", 1, -1, 0), ("x", 1, -1, 1, 1), ("mirror", 0, 0), ("mirror", 0, 1),
    ("mirror", 1, 0), ("y", 2, 4), ("mirror", 3, 0), ("own", 3, 1), ("mirror", 3, 1), ("own", 1, 1),
    ("mirror", 2, 0), ("mirror", 1, 1), ("own", 2, 1), ("mirror", 2, 1),
)


def kernel(
    row_labels_hbm, column_labels_hbm, integrals, amplitudes, occ_energy_hbm, vir_energy_hbm, out,
    packed, mirrored, plain, own, total, inverse, first, second, relay, landed_0, landed_1, landed_2, landed_3, occ_energy, vir_energy, occ_column, zeros,
    order_vmem, order, row_labels, column_labels, send_sems, recv_sems, local_sems,
):
    landed = (landed_0, landed_1, landed_2, landed_3)
    occ, vir = lax.axis_index("occ"), lax.axis_index("vir")
    core = occ % 2
    zh = (occ // 2) % NZ
    y = occ // (2 * NZ)
    zl = vir % 2
    x = vir // 2
    owner = zh != 3

    def at(dy=0, dz=0, sibling=False):
        c = 1 - core if sibling else core
        return (((y + dy + NY) % NY) * NZ + (zh + dz + NZ) % NZ) * 2 + c

    def vir_at(dx=0, other=False):
        return ((x + dx + NX) % NX) * 2 + (1 - zl if other else zl)

    def valid(stream):
        return (zh + stream) % NZ != 3

    names = {}
    pending = []

    def sem_of(name):
        return names.setdefault(name, len(names))

    def send(name, source, target, to_occ=None, to_vir=None, when=None):
        k = sem_of(name)

        def descriptor():
            return pltpu.make_async_remote_copy(
                src_ref=source(), dst_ref=target(), send_sem=send_sems.at[k], recv_sem=recv_sems.at[k],
                device_id=(occ if to_occ is None else to_occ, vir if to_vir is None else to_vir),
                device_id_type=MESH,
            )

        if when is None:
            descriptor().start()
            pending.append(lambda: descriptor().wait_send())
        else:
            pl.when(when)(lambda: descriptor().start())
            pending.append(lambda: pl.when(when)(lambda: descriptor().wait_send()))

    def arrived(name, target, when=None):
        k = sem_of(name)

        def wait():
            pltpu.make_async_remote_copy(
                src_ref=target(), dst_ref=target(), send_sem=send_sems.at[k], recv_sem=recv_sems.at[k],
                device_id=(at(sibling=True), vir), device_id_type=MESH,
            ).wait_recv()

        if when is None:
            wait()
        else:
            pl.when(when)(wait)

    def columns_of(t):
        return pl.ds(pl.multiple_of(512 * t, 512), 512)

    def send_first():
        for s in (1, 3, 2):
            t = (zh + s) % NZ
            send(("first", s), lambda t=t: integrals.at[:, columns_of(t)], lambda: first.at[zh], at(dz=s), when=t != 3)

    def unit(plane):
        rows = pl.ds(pl.multiple_of(16 * (plane % 2), 16), 16)
        return first.at[:, rows, pl.ds(pl.multiple_of(128 * (plane // 2), 128), 128)]

    def second_from(plane):
        return second.at[pl.ds(pl.multiple_of(4 * plane, 4), 4)]

    def on_first():
        for s in (1, 3, 2):
            arrived(("first", s), lambda s=s: first.at[(zh - s + NZ) % NZ], when=owner)

        @pl.when(owner)
        def _():
            pltpu.make_async_copy(integrals.at[:, columns_of(zh)], first.at[zh], local_sems.at[6]).wait()
            pltpu.make_async_copy(unit(y), second_from(y), local_sems.at[7]).start()

        for d in (4, 3, -3, 2, -2, 1, -1):
            plane = (y + d + NY) % NY
            send(("second", d), lambda p=plane: unit(p), lambda: second_from(y), at(dy=d), when=owner)

    def on_second():
        for d in (1, -1, 2, -2, 3, -3, 4):
            arrived(("second", d), lambda d=d: second_from((y - d + NY) % NY), when=owner)

        @pl.when(owner)
        def _():
            pltpu.make_async_copy(unit(y), second_from(y), local_sems.at[7]).wait()
            zero = jnp.broadcast_to(zeros[4 * zh + y // 2], (16, 128)) == 1
            columns = pl.ds(pl.multiple_of(128 * (4 * zh + y // 2), 128), 128)

            @pl.loop(0, 16)
            def _(p):
                a = second[order[0, p]].astype(jnp.float32)
                b = second[order[0, 16 + p]].astype(jnp.float32)
                packed[p, 2 * core + y % 2, :, columns] = jnp.where(zero, a, b).astype(jnp.bfloat16)

        for s in (3, 1):
            send(("z", s), slot(0, 0), slot(0, 0), at(dz=-s), when=owner)
        start_stream(0)
        send(("z", 2), slot(0, 0), slot(0, 0), at(dz=2), when=owner)

    def slot(delta, stream, half=None, sibling=False):
        def ref():
            plane, block = (y + delta + NY) % NY, (zh + stream) % NZ
            rows = slice(None) if half is None else pl.ds(8 * half, 8)
            columns = pl.ds(pl.multiple_of(128 * (4 * block + plane // 2), 128), 128)
            c = 1 - core if sibling else core
            return packed.at[rows, 2 * c + plane % 2, :, columns]

        return ref

    def half_of(distance, way):
        return None if distance < 4 else (0 if way > 0 else 1)

    def delta_of(distance, way):
        return 4 if distance == 4 else -way * distance

    def send_y(stream, distance, way):
        half = half_of(distance, way)
        ref = slot(delta_of(distance - 1, way), stream, half)
        send(("y", stream, distance, way), ref, ref, at(dy=way), when=valid(stream))

    def to_sibling(delta, stream):
        ref = slot(delta, stream)
        send(("sib", delta, stream), ref, ref, at(sibling=True), when=valid(stream))

    def start_stream(stream):
        send_y(stream, 1, 1)
        send_y(stream, 1, -1)
        to_sibling(0, stream)

    def on_z(stream):
        arrived(("z", stream), slot(0, stream), when=valid(stream))
        start_stream(stream)

    def on_y(stream, distance, way=None):
        for w in (1, -1) if way is None else (way,):
            ref = slot(delta_of(distance, w), stream, half_of(distance, w))
            arrived(("y", stream, distance, w), ref, when=valid(stream))
        if distance < 4:
            send_y(stream, distance + 1, way)
        to_sibling(delta_of(distance, way), stream)

    def index_of(way, part):
        return part + (0 if way > 0 else 2)

    def piece(dx, other, way, part):
        return lambda: mirrored.at[vir_at(dx, other), index_of(way, part)]

    def relay_of(way, part):
        return lambda: relay.at[index_of(way, part)]

    def landed_of(way, part):
        return lambda: landed[index_of(way, part)]

    def send_mirror(way, part):
        rows = pl.ds(16 * index_of(way, part), 16)
        send(("relay", way, part), lambda: plain.at[:, vir, rows], relay_of(way, part), at(dy=2 * way))

    def on_relay(way, part):
        arrived(("relay", way, part), relay_of(way, part))
        send(("mir", way, part), relay_of(way, part), landed_of(way, part), at(dy=2 * way))

    def to_x(other, way, part):
        ref = piece(0, other, way, part)
        for w in (1, -1):
            send(("x", other, way, part, w), ref, ref, to_vir=vir_at(w))

    def to_other(name, ref):
        send(name, ref, ref, to_vir=vir_at(0, True))

    def on_mir(way, part):
        arrived(("mir", way, part), landed_of(way, part))
        n = index_of(way, part)

        @pl.loop(0, 16, unroll=8)
        def _(b):
            lanes = pl.ds(pl.multiple_of(128 * b, 128), 128)
            mirrored[vir, n, :, lanes] = sorted_block(lambda i: landed[n][i], b, 16)

        if part == 0:
            to_x(0, way, part)
            to_other(("zl", way, part), piece(0, False, way, part))
        else:
            to_other(("zl", way, part), piece(0, False, way, part))
            to_x(0, way, part)

    def on_zl(way, part):
        arrived(("zl", way, part), piece(0, True, way, part))
        if part == 1:
            to_x(1, way, part)

    def on_x(other, way, part, w):
        if other and part == 0:
            arrived(("x", 1, way, part, w), piece(-w, True, way, part))
            return
        ref = piece(-w, other, way, part)
        arrived(("x", other, way, part, w), ref)
        if w == way:
            send(("xf", other, way, part), ref, ref, to_vir=vir_at(w))
        if part == 0:
            to_other(("x", 1, way, part, w), ref)

    def on_xf(other, way, part):
        ref = piece(2, other, way, part)
        arrived(("xf", other, way, part), ref)
        if part == 0 and not other:
            to_other(("xf", 1, way, part), ref)

    odd = y % 2
    needs = ((0, 1, -1, 2, -2), (3, -3, 4))

    def tiles_of(stream, half):
        steps = (((0, 0), (-1, 1)), ((1, -1), (2, 2)))[half]
        block = (zh + stream) % NZ
        return [4 * block + (y // 2 + jnp.where(odd == 1, o, e) + 4) % 4 for e, o in steps]

    def product(tiles, left):
        lanes = [pl.ds(pl.multiple_of(128 * t, 128), 128) for t in tiles]
        right = jnp.concatenate([packed[:, :, :, n].reshape(1024, 128) for n in lanes], axis=1)
        zero = jnp.concatenate([zeros[t] for t in tiles], axis=1) == 1
        a = jnp.dot(left(slice(0, 1024)), right, preferred_element_type=jnp.float32)
        b = jnp.dot(left(slice(1024, 2048)), right, preferred_element_type=jnp.float32)
        return jnp.where(zero, a, b)

    def on_inverse(part):
        @pl.loop(3 * part, 3 * part + 3)
        def _(t):
            inverse[t] = 1.0 / (vir_energy[pl.ds(t, 1), :] - occ_column[...])

    def on_own(stream, half):
        @pl.when(valid(stream))
        def _():
            for delta in needs[half]:
                arrived(("sib", delta, stream), slot(delta, stream, sibling=True))
            total[2 * stream + half] = product(tiles_of(stream, half), lambda lanes: own[:, lanes])

    def on_mirror(stream, half):
        @pl.when(valid(stream))
        def _():
            tiles = tiles_of(stream, half)
            value = total[2 * stream + half] - product(
                tiles, lambda lanes: mirrored[:, :, :, lanes].reshape(512, 1024)
            )
            for n, t in enumerate(tiles):
                columns = pl.ds(pl.multiple_of(128 * t, 128), 128)
                out[:, columns] = (value[:, 128 * n : 128 * n + 128] * inverse[t]).astype(jnp.bfloat16)

    def sorted_block(block, b, rows):
        low = lax.broadcasted_iota(jnp.int32, (rows, 128), 1) < TILE

        def tile(p, half):
            value = block(order[8, p]).astype(jnp.float32)
            there = jnp.broadcast_to(order[16, p], (rows, 128)) == half
            return jnp.where(there, value, pltpu.roll(value, TILE, 1))

        return jnp.where(low, tile(2 * b, 0), tile(2 * b + 1, 1)).astype(jnp.bfloat16)

    def on_sort(part):
        @pl.loop(2 * part, 2 * part + 2)
        def _(b):
            lanes = pl.ds(pl.multiple_of(128 * b, 128), 128)
            own[:, lanes] = sorted_block(lambda i: plain[i].reshape(512, 128), b, 512)

    def on_flush(rest):
        while len(pending) > rest:
            pending.pop(0)()

    def local(source, target, k):
        copy = pltpu.make_async_copy(source, target, local_sems.at[k])
        copy.start()
        return copy

    barrier = pltpu.get_barrier_semaphore()
    peers = [(at(dy=d), vir) for d in (1, -1, 2, -2, 3, -3, 4)] + [(at(dz=d), vir) for d in (1, -1, 2)]
    peers += [(at(sibling=True), vir), (occ, vir_at(0, True)), (occ, vir_at(1)), (occ, vir_at(-1))]
    for peer in peers:
        pl.semaphore_signal(barrier, inc=1, device_id=peer, device_id_type=MESH)

    labels_copies = [local(row_labels_hbm, row_labels, 0), local(column_labels_hbm, column_labels, 1)]
    plain_copies = [local(amplitudes.at[:, :, pl.ds(128 * b, 128)], plain.at[b], 8 + b) for b in range(16)]
    energy_copies = [local(occ_energy_hbm, occ_energy, 3), local(vir_energy_hbm, vir_energy, 4)]

    @pl.when(owner)
    def _():
        pltpu.make_async_copy(integrals.at[:, columns_of(zh)], first.at[zh], local_sems.at[6]).start()

    pl.semaphore_wait(barrier, len(peers))
    send_first()
    for copy in plain_copies:
        copy.wait()
    for part in (0, 1):
        for way in (1, -1):
            send_mirror(way, part)

    for copy in labels_copies:
        copy.wait()
    lane = lax.broadcasted_iota(jnp.int32, (8, 128), 1)
    places = [jnp.zeros((8, 128), jnp.int32)] * 3
    ones = jnp.int32(0)
    for r in range(32):
        label = row_labels[r]
        rank = jnp.minimum(jnp.where(label == 1, ones, r - ones), 15)
        here = lane == label * 16 + rank
        places = [jnp.where(here, n, place) for n, place in zip((r, r // 2, r % 2), places)]
        ones = ones + label
    for n in range(3):
        order_vmem[8 * n : 8 * n + 8, :] = places[n]
    order_copy = local(order_vmem, order, 2)

    side = lax.broadcasted_iota(jnp.int32, (1, 128), 1) < TILE
    for t in range(12):
        zeros[t] = jnp.where(jnp.where(side, column_labels[2 * t], column_labels[2 * t + 1]) == 0, 1, 0)
    for copy in energy_copies:
        copy.wait()
    for b in range(4):
        occ_column[128 * b : 128 * b + 128, :] = jnp.transpose(
            jnp.broadcast_to(occ_energy[b : b + 1, :], (128, 128))
        )
    order_copy.wait()

    handlers = {
        "a1": on_first, "a2": on_second, "z": on_z, "y": on_y, "relay": on_relay, "mir": on_mir,
        "zl": on_zl, "x": on_x, "xf": on_xf, "sort": on_sort, "inverse": on_inverse, "own": on_own,
        "mirror": on_mirror, "flush": on_flush,
    }
    for kind, *place in ORDER:
        handlers[kind](*place)
    on_flush(0)


def body(amplitudes, integrals, row_irreps, column_irreps, occ_energy, vir_energy):
    hbm = pl.BlockSpec(memory_space=pltpu.HBM)
    return pl.pallas_call(
        kernel,
        out_shape=pltpu.VMEM((512, 1536), jnp.bfloat16),
        in_specs=[hbm] * 6,
        out_specs=pl.BlockSpec(memory_space=pltpu.VMEM),
        scratch_shapes=[
            pltpu.VMEM((16, 4, 16, 1536), jnp.bfloat16),
            pltpu.VMEM((8, 4, 16, 2048), jnp.bfloat16),
            pltpu.VMEM((16, 8, 64, 128), jnp.bfloat16),
            pltpu.VMEM((512, 2048), jnp.bfloat16),
            pltpu.VMEM((8, 512, 256), jnp.float32),
            pltpu.VMEM((12, 512, 128), jnp.float32),
            pltpu.VMEM((4, 32, 512), jnp.bfloat16),
            pltpu.VMEM((32, 16, 128), jnp.bfloat16),
            pltpu.VMEM((4, 16, 16, 128), jnp.bfloat16),
            *[pltpu.VMEM((16, 16, 128), jnp.bfloat16)] * 4,
            pltpu.VMEM((4, 128), jnp.float32),
            pltpu.VMEM((12, 128), jnp.float32),
            pltpu.VMEM((512, 128), jnp.float32),
            pltpu.VMEM((12, 1, 128), jnp.int32),
            pltpu.VMEM((24, 128), jnp.int32),
            pltpu.SMEM((24, 128), jnp.int32),
            pltpu.SMEM((32,), jnp.int32),
            pltpu.SMEM((24,), jnp.int32),
            pltpu.SemaphoreType.DMA((N_SEMS,)),
            pltpu.SemaphoreType.DMA((N_SEMS,)),
            pltpu.SemaphoreType.DMA((24,)),
        ],
        compiler_params=pltpu.CompilerParams(
            collective_id=0, has_side_effects=True, vmem_limit_bytes=58 * 2**20
        ),
        cost_estimate=pl.CostEstimate(flops=6442450944, bytes_accessed=4 * 2**20, transcendentals=0),
    )(
        row_irreps, column_irreps, integrals, amplitudes.reshape(8, 64, 2048),
        occ_energy.reshape(4, 128), vir_energy.reshape(12, 128),
    )


def solution(mesh):
    placed = (P("occ", None), P("occ", "vir"), P(), P("vir"), P("occ"), P("vir"))
    return jax.shard_map(
        body, mesh=mesh, in_specs=placed, out_specs=P("occ", "vir"), check_vma=False
    )
```

```python
import jax
import jax.numpy as jnp
from jax import lax
from jax.experimental import pallas as pl
from jax.experimental.pallas import tpu as pltpu
from jax.sharding import PartitionSpec as P

TILE = 64
MESH = pl.DeviceIdType.MESH
NY, NZ, NX = 8, 4, 4
DELTAS = (0, 1, -1, 2, -2, 3, -3, 4)
N_SEMS = 128
ORDER = (
    ("sort", 4), ("sort", 7), ("sort", 6), ("sort", 1), ("sort", 0), ("a1",), ("inverse", 3), ("relay", 1, 0),
    ("relay", -1, 0), ("relay", 1, 1), ("a2",), ("relay", -1, 1), ("mir", 1, 0),
    ("inverse", 1), ("inverse", 2), ("mir", -1, 0), ("sort", 3), ("z", 3), ("mir", 1, 1), ("z", 1),
    ("y", 0, 1, -1), ("flush", 30), ("y", 0, 1, 1), ("mir", -1, 1), ("x", 0, 1, 0, -1), ("z", 2),
    ("flush", 30), ("y", 3, 1, -1), ("x", 0, -1, 0, -1), ("y", 3, 1, 1), ("sort", 2), ("flush", 30),
    ("y", 1, 1, -1), ("y", 1, 1, 1), ("zl", -1, 0), ("x", 0, 1, 0, 1), ("y", 0, 2, 1), ("y", 0, 2, -1),
    ("zl", 1, 0), ("flush", 30), ("zl", 1, 1), ("x", 0, 1, 1, 1), ("inverse", 0), ("x", 0, -1, 1, 1),
    ("y", 2, 1, -1), ("y", 2, 1, 1), ("flush", 30), ("y", 3, 2, 1), ("zl", -1, 1), ("x", 0, 1, 1, -1),
    ("x", 0, -1, 1, -1), ("y", 3, 2, -1), ("flush", 30), ("y", 1, 2, -1), ("xf", 0, 1, 0), ("y", 1, 2, 1),
    ("y", 0, 3, 1), ("x", 0, -1, 0, 1), ("y", 0, 3, -1), ("sort", 5), ("flush", 30), ("y", 2, 2, 1),
    ("x", 1, 1, 1, 1), ("xf", 0, -1, 0), ("y", 2, 2, -1), ("own", 0, 0), ("own", 1, 0), ("y", 3, 3, 1),
    ("y", 3, 3, -1), ("x", 1, 1, 1, -1), ("x", 1, -1, 1, -1), ("flush", 30), ("y", 1, 3, 1),
    ("y", 1, 3, -1), ("x", 1, -1, 0, -1), ("y", 0, 4), ("own", 2, 0), ("x", 1, 1, 0, -1), ("xf", 1, 1, 0),
    ("flush", 30), ("y", 2, 3, 1), ("y", 2, 3, -1), ("xf", 0, 1, 1), ("xf", 0, -1, 1), ("x", 1, -1, 0, 1),
    ("y", 3, 4), ("own", 3, 0), ("xf", 1, 1, 1), ("y", 1, 4), ("own", 0, 1), ("x", 1, 1, 0, 1),
    ("xf", 1, -1, 1), ("xf", 1, -1, 0), ("x", 1, -1, 1, 1), ("mirror", 0, 0), ("mirror", 0, 1),
    ("mirror", 1, 0), ("y", 2, 4), ("mirror", 3, 0), ("full", 3, 1),     ("mirror", 2, 0), ("full", 1, 1), ("full", 2, 1),
)


def kernel(
    row_labels_hbm, column_labels_hbm, integrals, amplitudes, occ_energy_hbm, vir_energy_hbm, out,
    packed, mirrored, plain, eighth, own, total, inverse, first, second, relay, landed_0, landed_1, landed_2, landed_3, occ_energy, vir_energy, occ_column, zeros,
    order_vmem, order, row_labels, column_labels, send_sems, recv_sems, local_sems,
):
    landed = (landed_0, landed_1, landed_2, landed_3)
    occ, vir = lax.axis_index("occ"), lax.axis_index("vir")
    core = occ % 2
    zh = (occ // 2) % NZ
    y = occ // (2 * NZ)
    zl = vir % 2
    x = vir // 2
    owner = zh != 3

    def at(dy=0, dz=0, sibling=False):
        c = 1 - core if sibling else core
        return (((y + dy + NY) % NY) * NZ + (zh + dz + NZ) % NZ) * 2 + c

    def vir_at(dx=0, other=False):
        return ((x + dx + NX) % NX) * 2 + (1 - zl if other else zl)

    def valid(stream):
        return (zh + stream) % NZ != 3

    names = {}
    pending = []

    def sem_of(name):
        return names.setdefault(name, len(names))

    def send(name, source, target, to_occ=None, to_vir=None, when=None):
        k = sem_of(name)

        def descriptor():
            return pltpu.make_async_remote_copy(
                src_ref=source(), dst_ref=target(), send_sem=send_sems.at[k], recv_sem=recv_sems.at[k],
                device_id=(occ if to_occ is None else to_occ, vir if to_vir is None else to_vir),
                device_id_type=MESH,
            )

        if when is None:
            descriptor().start()
            pending.append(lambda: descriptor().wait_send())
        else:
            pl.when(when)(lambda: descriptor().start())
            pending.append(lambda: pl.when(when)(lambda: descriptor().wait_send()))

    def arrived(name, target, when=None):
        k = sem_of(name)

        def wait():
            pltpu.make_async_remote_copy(
                src_ref=target(), dst_ref=target(), send_sem=send_sems.at[k], recv_sem=recv_sems.at[k],
                device_id=(at(sibling=True), vir), device_id_type=MESH,
            ).wait_recv()

        if when is None:
            wait()
        else:
            pl.when(when)(wait)

    def columns_of(t):
        return pl.ds(pl.multiple_of(512 * t, 512), 512)

    def send_first():
        for s in (1, 3, 2):
            t = (zh + s) % NZ
            send(("first", s), lambda t=t: integrals.at[:, columns_of(t)], lambda: first.at[zh], at(dz=s), when=t != 3)

    def unit(plane):
        rows = pl.ds(pl.multiple_of(16 * (plane % 2), 16), 16)
        return first.at[:, rows, pl.ds(pl.multiple_of(128 * (plane // 2), 128), 128)]

    def second_from(plane):
        return second.at[pl.ds(pl.multiple_of(4 * plane, 4), 4)]

    def on_first():
        for s in (1, 3, 2):
            arrived(("first", s), lambda s=s: first.at[(zh - s + NZ) % NZ], when=owner)

        @pl.when(owner)
        def _():
            pltpu.make_async_copy(integrals.at[:, columns_of(zh)], first.at[zh], local_sems.at[6]).wait()
            pltpu.make_async_copy(unit(y), second_from(y), local_sems.at[7]).start()

        for d in (4, 3, -3, 2, -2, 1, -1):
            plane = (y + d + NY) % NY
            send(("second", d), lambda p=plane: unit(p), lambda: second_from(y), at(dy=d), when=owner)

    def on_second():
        for d in (1, -1, 2, -2, 3, -3, 4):
            arrived(("second", d), lambda d=d: second_from((y - d + NY) % NY), when=owner)

        @pl.when(owner)
        def _():
            pltpu.make_async_copy(unit(y), second_from(y), local_sems.at[7]).wait()
            zero = jnp.broadcast_to(zeros[4 * zh + y // 2], (16, 128)) == 1
            columns = pl.ds(pl.multiple_of(128 * (4 * zh + y // 2), 128), 128)

            @pl.loop(0, 16)
            def _(p):
                a = second[order[0, p]].astype(jnp.float32)
                b = second[order[0, 16 + p]].astype(jnp.float32)
                packed[p, 2 * core + y % 2, :, columns] = jnp.where(zero, a, b).astype(jnp.bfloat16)

        for s in (3, 1):
            send(("z", s), slot(0, 0), slot(0, 0), at(dz=-s), when=owner)
        start_stream(0)
        send(("z", 2), slot(0, 0), slot(0, 0), at(dz=2), when=owner)

    def slot(delta, stream, half=None, sibling=False):
        def ref():
            plane, block = (y + delta + NY) % NY, (zh + stream) % NZ
            rows = slice(None) if half is None else pl.ds(8 * half, 8)
            columns = pl.ds(pl.multiple_of(128 * (4 * block + plane // 2), 128), 128)
            c = 1 - core if sibling else core
            return packed.at[rows, 2 * c + plane % 2, :, columns]

        return ref

    def half_of(distance, way):
        return None if distance < 4 else (0 if way > 0 else 1)

    def delta_of(distance, way):
        return 4 if distance == 4 else -way * distance

    def send_y(stream, distance, way):
        half = half_of(distance, way)
        ref = slot(delta_of(distance - 1, way), stream, half)
        send(("y", stream, distance, way), ref, ref, at(dy=way), when=valid(stream))

    def to_sibling(delta, stream):
        ref = slot(delta, stream)
        send(("sib", delta, stream), ref, ref, at(sibling=True), when=valid(stream))

    def start_stream(stream):
        send_y(stream, 1, 1)
        send_y(stream, 1, -1)
        to_sibling(0, stream)

    def on_z(stream):
        arrived(("z", stream), slot(0, stream), when=valid(stream))
        start_stream(stream)

    def on_y(stream, distance, way=None):
        for w in (1, -1) if way is None else (way,):
            ref = slot(delta_of(distance, w), stream, half_of(distance, w))
            arrived(("y", stream, distance, w), ref, when=valid(stream))
        if distance < 4:
            send_y(stream, distance + 1, way)
        to_sibling(delta_of(distance, way), stream)

    def index_of(way, part):
        return part + (0 if way > 0 else 2)

    def piece(dx, other, way, part):
        return lambda: mirrored.at[vir_at(dx, other), index_of(way, part)]

    def relay_of(way, part):
        return lambda: relay.at[index_of(way, part)]

    def landed_of(way, part):
        return lambda: landed[index_of(way, part)]

    def send_mirror(way, part):
        rows = pl.ds(16 * index_of(way, part), 16)
        send(("relay", way, part), lambda: eighth.at[:, rows], relay_of(way, part), at(dy=2 * way))

    def on_relay(way, part):
        arrived(("relay", way, part), relay_of(way, part))
        send(("mir", way, part), relay_of(way, part), landed_of(way, part), at(dy=2 * way))

    def to_x(other, way, part):
        ref = piece(0, other, way, part)
        for w in (1, -1):
            send(("x", other, way, part, w), ref, ref, to_vir=vir_at(w))

    def to_other(name, ref):
        send(name, ref, ref, to_vir=vir_at(0, True))

    def on_mir(way, part):
        arrived(("mir", way, part), landed_of(way, part))
        n = index_of(way, part)

        @pl.loop(0, 16, unroll=8)
        def _(b):
            lanes = pl.ds(pl.multiple_of(128 * b, 128), 128)
            mirrored[vir, n, :, lanes] = sorted_block(lambda i: landed[n][i], b, 16)

        if part == 0:
            to_x(0, way, part)
            to_other(("zl", way, part), piece(0, False, way, part))
        else:
            to_other(("zl", way, part), piece(0, False, way, part))
            to_x(0, way, part)

    def on_zl(way, part):
        arrived(("zl", way, part), piece(0, True, way, part))
        if part == 1:
            to_x(1, way, part)

    def on_x(other, way, part, w):
        if other and part == 0:
            arrived(("x", 1, way, part, w), piece(-w, True, way, part))
            return
        ref = piece(-w, other, way, part)
        arrived(("x", other, way, part, w), ref)
        if w == way:
            send(("xf", other, way, part), ref, ref, to_vir=vir_at(w))
        if part == 0:
            to_other(("x", 1, way, part, w), ref)

    def on_xf(other, way, part):
        ref = piece(2, other, way, part)
        arrived(("xf", other, way, part), ref)
        if part == 0 and not other:
            to_other(("xf", 1, way, part), ref)

    odd = y % 2
    needs = ((0, 1, -1, 2, -2), (3, -3, 4))

    def tiles_of(stream, half):
        steps = (((0, 0), (-1, 1)), ((1, -1), (2, 2)))[half]
        block = (zh + stream) % NZ
        return [4 * block + (y // 2 + jnp.where(odd == 1, o, e) + 4) % 4 for e, o in steps]

    def product(tiles, *lefts):
        lanes = [pl.ds(pl.multiple_of(128 * t, 128), 128) for t in tiles]
        right = jnp.concatenate([packed[:, :, :, n].reshape(1024, 128) for n in lanes], axis=1)
        zero = jnp.concatenate([zeros[t] for t in tiles], axis=1) == 1

        def of_label(part):
            first, *rest = [jnp.dot(left(part), right, preferred_element_type=jnp.float32) for left in lefts]
            return first - rest[0] if rest else first

        return jnp.where(zero, of_label(slice(0, 1024)), of_label(slice(1024, 2048)))

    def own_rows(part):
        return own[:, part]

    def mirrored_rows(part):
        return mirrored[:, :, :, part].reshape(512, 1024)

    def store(tiles, value):
        for n, t in enumerate(tiles):
            columns = pl.ds(pl.multiple_of(128 * t, 128), 128)
            out[:, columns] = (value[:, 128 * n : 128 * n + 128] * inverse[t]).astype(jnp.bfloat16)

    def on_inverse(part):
        @pl.loop(3 * part, 3 * part + 3)
        def _(t):
            inverse[t] = 1.0 / (vir_energy[pl.ds(t, 1), :] - occ_column[...])

    def wait_siblings(stream, half):
        for delta in needs[half]:
            arrived(("sib", delta, stream), slot(delta, stream, sibling=True))

    def on_own(stream, half):
        @pl.when(valid(stream))
        def _():
            wait_siblings(stream, half)
            total[2 * stream + half] = product(tiles_of(stream, half), own_rows)

    def on_mirror(stream, half):
        @pl.when(valid(stream))
        def _():
            tiles = tiles_of(stream, half)
            store(tiles, total[2 * stream + half] - product(tiles, mirrored_rows))

    def on_full(stream, half):
        @pl.when(valid(stream))
        def _():
            wait_siblings(stream, half)
            tiles = tiles_of(stream, half)
            store(tiles, product(tiles, own_rows, mirrored_rows))

    def sorted_block(block, b, rows):
        low = lax.broadcasted_iota(jnp.int32, (rows, 128), 1) < TILE

        def tile(p, half):
            value = block(order[8, p]).astype(jnp.float32)
            there = jnp.broadcast_to(order[16, p], (rows, 128)) == half
            return jnp.where(there, value, pltpu.roll(value, TILE, 1))

        return jnp.where(low, tile(2 * b, 0), tile(2 * b + 1, 1)).astype(jnp.bfloat16)

    def on_sort(part):
        @pl.loop(2 * part, 2 * part + 2)
        def _(b):
            lanes = pl.ds(pl.multiple_of(128 * b, 128), 128)
            own[:, lanes] = sorted_block(lambda i: plain[i].reshape(512, 128), b, 512)

    def on_flush(rest):
        while len(pending) > rest:
            pending.pop(0)()

    def local(source, target, k):
        copy = pltpu.make_async_copy(source, target, local_sems.at[k])
        copy.start()
        return copy

    barrier = pltpu.get_barrier_semaphore()
    peers = [(at(dy=d), vir) for d in (1, -1, 2, -2, 3, -3, 4)] + [(at(dz=d), vir) for d in (1, -1, 2)]
    peers += [(at(sibling=True), vir), (occ, vir_at(0, True)), (occ, vir_at(1)), (occ, vir_at(-1))]
    for peer in peers:
        pl.semaphore_signal(barrier, inc=1, device_id=peer, device_id_type=MESH)

    eighth_copies = [local(amplitudes.at[vir, :, pl.ds(128 * b, 128)], eighth.at[b], 24 + b) for b in range(16)]
    labels_copies = [local(row_labels_hbm, row_labels, 0), local(column_labels_hbm, column_labels, 1)]
    energy_copies = [local(occ_energy_hbm, occ_energy, 3), local(vir_energy_hbm, vir_energy, 4)]

    @pl.when(owner)
    def _():
        pltpu.make_async_copy(integrals.at[:, columns_of(zh)], first.at[zh], local_sems.at[6]).start()

    pl.semaphore_wait(barrier, len(peers))
    send_first()
    for copy in eighth_copies:
        copy.wait()
    for part in (0, 1):
        for way in (1, -1):
            send_mirror(way, part)
    plain_copies = [local(amplitudes.at[:, :, pl.ds(128 * b, 128)], plain.at[b], 8 + b) for b in range(16)]

    for copy in labels_copies:
        copy.wait()
    lane = lax.broadcasted_iota(jnp.int32, (8, 128), 1)
    places = [jnp.zeros((8, 128), jnp.int32)] * 3
    ones = jnp.int32(0)
    for r in range(32):
        label = row_labels[r]
        rank = jnp.minimum(jnp.where(label == 1, ones, r - ones), 15)
        here = lane == label * 16 + rank
        places = [jnp.where(here, n, place) for n, place in zip((r, r // 2, r % 2), places)]
        ones = ones + label
    for n in range(3):
        order_vmem[8 * n : 8 * n + 8, :] = places[n]
    order_copy = local(order_vmem, order, 2)

    side = lax.broadcasted_iota(jnp.int32, (1, 128), 1) < TILE
    for t in range(12):
        zeros[t] = jnp.where(jnp.where(side, column_labels[2 * t], column_labels[2 * t + 1]) == 0, 1, 0)
    for copy in energy_copies:
        copy.wait()
    for b in range(4):
        occ_column[128 * b : 128 * b + 128, :] = jnp.transpose(
            jnp.broadcast_to(occ_energy[b : b + 1, :], (128, 128))
        )
    order_copy.wait()
    for copy in plain_copies:
        copy.wait()

    handlers = {
        "a1": on_first, "a2": on_second, "z": on_z, "y": on_y, "relay": on_relay, "mir": on_mir,
        "zl": on_zl, "x": on_x, "xf": on_xf, "sort": on_sort, "inverse": on_inverse, "own": on_own,
        "mirror": on_mirror, "full": on_full, "flush": on_flush,
    }
    for kind, *place in ORDER:
        handlers[kind](*place)
    on_flush(0)


def body(amplitudes, integrals, row_irreps, column_irreps, occ_energy, vir_energy):
    hbm = pl.BlockSpec(memory_space=pltpu.HBM)
    return pl.pallas_call(
        kernel,
        out_shape=pltpu.VMEM((512, 1536), jnp.bfloat16),
        in_specs=[hbm] * 6,
        out_specs=pl.BlockSpec(memory_space=pltpu.VMEM),
        scratch_shapes=[
            pltpu.VMEM((16, 4, 16, 1536), jnp.bfloat16),
            pltpu.VMEM((8, 4, 16, 2048), jnp.bfloat16),
            pltpu.VMEM((16, 8, 64, 128), jnp.bfloat16),
            pltpu.VMEM((16, 64, 128), jnp.bfloat16),
            pltpu.VMEM((512, 2048), jnp.bfloat16),
            pltpu.VMEM((8, 512, 256), jnp.float32),
            pltpu.VMEM((12, 512, 128), jnp.float32),
            pltpu.VMEM((4, 32, 512), jnp.bfloat16),
            pltpu.VMEM((32, 16, 128), jnp.bfloat16),
            pltpu.VMEM((4, 16, 16, 128), jnp.bfloat16),
            *[pltpu.VMEM((16, 16, 128), jnp.bfloat16)] * 4,
            pltpu.VMEM((4, 128), jnp.float32),
            pltpu.VMEM((12, 128), jnp.float32),
            pltpu.VMEM((512, 128), jnp.float32),
            pltpu.VMEM((12, 1, 128), jnp.int32),
            pltpu.VMEM((24, 128), jnp.int32),
            pltpu.SMEM((24, 128), jnp.int32),
            pltpu.SMEM((32,), jnp.int32),
            pltpu.SMEM((24,), jnp.int32),
            pltpu.SemaphoreType.DMA((N_SEMS,)),
            pltpu.SemaphoreType.DMA((N_SEMS,)),
            pltpu.SemaphoreType.DMA((40,)),
        ],
        compiler_params=pltpu.CompilerParams(
            collective_id=0, has_side_effects=True, vmem_limit_bytes=58 * 2**20
        ),
        cost_estimate=pl.CostEstimate(flops=6442450944, bytes_accessed=4 * 2**20, transcendentals=0),
    )(
        row_irreps, column_irreps, integrals, amplitudes.reshape(8, 64, 2048),
        occ_energy.reshape(4, 128), vir_energy.reshape(12, 128),
    )


def solution(mesh):
    placed = (P("occ", None), P("occ", "vir"), P(), P("vir"), P("occ"), P("vir"))
    return jax.shard_map(
        body, mesh=mesh, in_specs=placed, out_specs=P("occ", "vir"), check_vma=False
    )
```
